256 devices in a mesh: dp: 16 (over x, y), enc: 16 (over z, core).
Axes of the slice: x: 4, y: 4, z: 8, core: 2. Of those that a mesh axis runs over, the one named last changes fastest.
Arguments:
- targets: bfloat16 [16384, 4096], P('enc', 'dp'), may hold values from -6 to 6
- encoded: bfloat16 [2048, 4096], P('enc', 'dp'), may hold values from -70 to 70
- norm_gain: float32 [4096], replicated, may hold values from 0.1 to 1.9
- query_weight: bfloat16 [4096, 4096], P(None, 'dp'), may hold values from -0.005859375 to 0.005859375
- key_weight: bfloat16 [4096, 4096], P(None, 'dp'), may hold values from -0.09375 to 0.09375
- value_weight: bfloat16 [4096, 4096], P(None, 'dp'), may hold values from -0.09375 to 0.09375
- output_weight: bfloat16 [4096, 4096], P('dp'), may hold values from -0.09375 to 0.09375
- target_segment: int32 [16384], replicated, may hold values from 0 to 63, never falling along the last dimension, each value on 1 to 512 neighbouring positions
- encoder_segment: int32 [2048], replicated, may hold values from 0 to 63, as said below
- tile_slot: int32 [128], replicated, may hold values from 0 to 127, as said below
Outputs:
- attended: bfloat16 [16384, 4096], P('enc', 'dp')
The draws below stay inside these ranges and needn't reach their ends.
Inputs may be any that keep to these rules, and one draw needn't show every extreme that they name: `target_segment`: never falling; every segment 0 to 63 holds target tokens and encoder tokens both; some segment has exactly 512 target tokens. `encoder_segment`: each segment's encoder tokens stand together in one run, every segment has one; some segment has exactly 256 encoder tokens. `tile_slot`: each slot once; the 8 tiles of one index of enc go to 8 different owners, so every owner receives exactly one tile from each of 8 different indices of enc.
All inputs are finite; a program needn't handle non-finite values.
Results may differ from the reference program's by a relative error of at most 0.019.
Values may be sent and summed in bfloat16 or wider, within the bound.
A program may use at most 128 MiB of HBM per device.

```python
import math
import jax
import jax.numpy as jnp
import numpy as np
from jax import lax

D = 4096
H = 16
HD = 256
TILE = 128
TILES_DEV = 8
TILES = 128
TGT = 16384
ENC = 2048
SEGS = 64
TGT_MOST = 512


def draw_encoded(key, part):
    base = jax.random.normal(jax.random.fold_in(key, 1), (ENC, D), jnp.float32)
    return jnp.clip(base, -6.0, 6.0).astype(jnp.bfloat16)


def draw_encoder_segment(key, part):
    key = jax.random.fold_in(key, 21)
    base_len = ENC // SEGS
    pair_count = SEGS // 2
    shifts = jax.random.randint(jax.random.fold_in(key, 1), (pair_count,), -(base_len // 2), base_len // 2 + 1).astype(jnp.int32)
    paired = jnp.stack((base_len + shifts, base_len - shifts), axis=1).reshape(SEGS).astype(jnp.int32)
    group_start = (jax.random.randint(jax.random.fold_in(key, 2), (), 0, SEGS // 16) * 16).astype(jnp.int32)
    pattern = jnp.concatenate((jnp.full((1,), 8 * base_len, jnp.int32), jnp.full((7,), base_len, jnp.int32), jnp.full((8,), base_len // 8, jnp.int32)))
    index = jnp.arange(SEGS, dtype=jnp.int32)
    inside = (index >= group_start) & (index < group_start + 16)
    within = jnp.clip(index - group_start, 0, 15)
    lengths = jnp.where(inside, pattern[within], paired).astype(jnp.int32)
    ends = jnp.cumsum(lengths).astype(jnp.int32)
    tokens = jnp.arange(ENC, dtype=jnp.int32)
    drawn = jnp.sum((tokens[:, None] >= ends[None, :]).astype(jnp.int32), axis=1).astype(jnp.int32)
    return ((drawn + SEGS // 2) % SEGS).astype(jnp.int32)


def owner_orders(key, count, length):
    return jax.vmap(lambda owner_index: jax.random.permutation(jax.random.fold_in(key, owner_index), length))(jnp.arange(count, dtype=jnp.int32))


def draw_tile_slot(key, part):
    owners = TILES // TILES_DEV
    owner_order = jax.random.permutation(jax.random.fold_in(key, 11), owners).astype(jnp.int32)
    offsets = jax.random.permutation(jax.random.fold_in(key, 12), owners)[:TILES_DEV].astype(jnp.int32)
    sources = jnp.arange(TILES, dtype=jnp.int32) // TILES_DEV
    within = jnp.arange(TILES, dtype=jnp.int32) % TILES_DEV
    shuffled = owner_orders(jax.random.fold_in(key, 13), owners, TILES_DEV).astype(jnp.int32)
    channel = shuffled[sources, within]
    target_owner = owner_order[(sources + offsets[channel]) % owners]
    places = owner_orders(jax.random.fold_in(key, 14), owners, TILES_DEV).astype(jnp.int32)
    position = places[target_owner, channel]
    return (target_owner * TILES_DEV + position).astype(jnp.int32)


def block_scale(own_key, dims, pieces, smallest, high):
    def one(axis_at, parts):
        heights = jax.random.uniform(jax.random.fold_in(jax.random.fold_in(own_key, 6), axis_at), (parts,), jnp.float32, smallest / len(pieces), high / len(pieces))
        return jnp.repeat(jnp.exp(heights), dims[axis_at] // parts).reshape((-1,) + (1,) * (len(dims) - axis_at - 1))

    level = one(*pieces[0])
    for cut in pieces[1:]:
        level = level * one(*cut)
    return level


def profile(number_of, total, limit, slope):
    loads = [(1 << 20) // math.isqrt(standing ** slope) + 1 for standing in range(2, number_of + 1)]
    rest, holding = total - limit - (number_of - 1), [1] * (number_of - 1)
    while rest > 0:
        candidates = [i for i in range(number_of - 1) if holding[i] < limit]
        pool, left = sum([loads[i] for i in candidates]), rest
        for i in candidates:
            addition = min(limit - holding[i], max(1, left * loads[i] // pool), rest)
            holding[i] = holding[i] + addition
            rest = rest - addition
    return np.array([limit] + holding)


def uneven(stream_key, count, total, reach, skew):
    if count == 2:
        one = jax.random.randint(stream_key, (), max(1, total - reach), min(reach, total - 1) + 1)
        return jnp.stack([one, total - one])
    tallies = jnp.asarray(profile(count, total, reach, skew), jnp.int32)
    twos = (count - 1) // 2
    giver, taker = tallies[1:1 + 2 * twos:2], tallies[2:2 + 2 * twos:2]
    slack = jnp.minimum(giver - 1, reach - taker)
    moved = jax.random.randint(jax.random.fold_in(stream_key, 1), (twos,), 0, 1 << 20) % (slack + 1)
    tallies = tallies.at[1:1 + 2 * twos:2].set(giver - moved).at[2:2 + 2 * twos:2].set(taker + moved)
    return tallies[jax.random.permutation(jax.random.fold_in(stream_key, 2), count)]


def normal_values(stream_key, extent, scale, limit, split=(), kind=jnp.bfloat16):
    values = scale * jax.random.normal(stream_key, extent, jnp.float32)
    if split:
        values = values * block_scale(stream_key, extent, split, -0.22, 0.18)
    return jnp.clip(values, -limit, limit).astype(kind)


def setup_inputs(seed: int = 0) -> dict:
    key_list = jax.random.split(jax.random.key(seed), 11)
    return {
        "targets": normal_values(key_list[0], (TGT, D), 1.0, 6.0, ((0, 16), (1, 16))),
        "encoded": draw_encoded(jax.random.fold_in(key_list[10], 71), 0),
        "norm_gain": jnp.clip(1.0 + 0.18 * jax.random.normal(key_list[2], (D,), jnp.float32), 0.1, 1.9),
        "query_weight": normal_values(key_list[3], (D, H * HD), (D * HD) ** -0.5, 0.005859375, ((1, 16),)),
        "key_weight": normal_values(key_list[4], (D, H * HD), D ** -0.5, 0.09375, ((1, 16),)),
        "value_weight": normal_values(key_list[5], (D, H * HD), D ** -0.5, 0.09375, ((1, 16),)),
        "output_weight": normal_values(key_list[6], (H * HD, D), (H * HD) ** -0.5, 0.09375, ((0, 16),)),
        "target_segment": jnp.searchsorted(jnp.cumsum(uneven(key_list[7], SEGS, TGT, TGT_MOST, 2)), jnp.arange(TGT), side="right").astype(jnp.int32),
        "encoder_segment": draw_encoder_segment(jax.random.fold_in(key_list[10], 71), 0),
        "tile_slot": draw_tile_slot(jax.random.fold_in(key_list[10], 71), 0),
    }


def reference(targets, encoded, norm_gain, query_weight, key_weight, value_weight, output_weight, target_segment, encoder_segment, tile_slot):
    widened = targets.astype(jnp.float32)
    inverse_rms = lax.rsqrt(lax.optimization_barrier(jnp.mean(widened * widened, axis=-1, keepdims=True)) + 1e-06)
    normed = (widened * inverse_rms * norm_gain).astype(jnp.bfloat16)
    queries = jnp.dot(normed, query_weight, preferred_element_type=jnp.float32).astype(jnp.bfloat16)
    key_rows = jnp.dot(encoded, key_weight, preferred_element_type=jnp.float32).astype(jnp.bfloat16)
    value_rows = jnp.dot(encoded, value_weight, preferred_element_type=jnp.float32).astype(jnp.bfloat16)
    allowed = target_segment[:, None] == encoder_segment[None, :]

    def one_head(head_index):
        offset = (head_index * HD).astype(jnp.int32)
        query_head = lax.dynamic_slice_in_dim(queries, offset, HD, 1)
        key_head = lax.dynamic_slice_in_dim(key_rows, offset, HD, 1)
        value_head = lax.dynamic_slice_in_dim(value_rows, offset, HD, 1)
        scores = jnp.dot(query_head, key_head.T, preferred_element_type=jnp.float32)
        scores = jnp.where(allowed, scores, -1e+30)
        row_max = lax.optimization_barrier(jnp.max(scores, axis=-1, keepdims=True))
        weights = jnp.where(allowed, jnp.exp(scores - row_max), 0.0)
        denominator = lax.optimization_barrier(jnp.sum(weights, axis=-1, keepdims=True))
        summed = jnp.dot(weights.astype(jnp.bfloat16), value_head, preferred_element_type=jnp.float32)
        return (summed / denominator).astype(jnp.bfloat16)
    per_head = lax.map(one_head, jnp.arange(H, dtype=jnp.int32))
    context = jnp.transpose(per_head, (1, 0, 2)).reshape(TGT, H * HD)
    tiles = context.reshape(TILES, TILE, H * HD)
    routed = jnp.zeros_like(tiles).at[tile_slot].set(tiles).reshape(TGT, H * HD)
    return jnp.dot(routed, output_weight, preferred_element_type=jnp.float32).astype(jnp.bfloat16)
```

```python
import jax
import jax.numpy as jnp
from jax import lax
from jax.experimental import pallas as pl
from jax.experimental.pallas import tpu as pltpu
from jax.sharding import PartitionSpec as P

HD = 256
TILE = 128
TILES = 8
HALF = TILE // 2
SIDE = 4
DEPTH = 8
ENC_PEERS = 16
FEATURES = 4096
BF = jnp.bfloat16
F32 = jnp.float32


def kernel(
    targets,
    encoded,
    gain,
    query_weight,
    key_weight,
    value_weight,
    output_weight,
    target_segment,
    encoder_segment,
    slot_row,
    slot,
    out,
    own_targets,
    sent_tiles,
    came_tiles,
    enc_all,
    weight_k,
    weight_v,
    weight_q,
    weight_o,
    kv,
    squares,
    rows_q,
    rows_o,
    kept_q,
    kept_o,
    far_q,
    far_o,
    half_q,
    half_o,
    near_q,
    near_o,
    sum_q,
    sum_o,
    out_rows,
    local_sem,
    enc_sem,
    tile_sem,
    wq_sem,
    wo_sem,
    pair_sem,
    kv_sem,
    kvp_sem,
    sq_sem,
    gather_q_sem,
    gather_o_sem,
    pass_q_sem,
    pass_o_sem,
    far_q_sem,
    far_o_sem,
    near_q_sem,
    near_o_sem,
    out_sem,
):
    dp = lax.axis_index("dp")
    e = lax.axis_index("enc")
    x, y = dp // SIDE, dp % SIDE
    z, c = e // 2, e % 2

    def device(dx=0, dy=0, dz=0, dc=0):
        return (
            ((x + dx + SIDE) % SIDE) * SIDE + (y + dy + SIDE) % SIDE,
            ((z + dz + DEPTH) % DEPTH) * 2 + (c + dc) % 2,
        )

    def remote(src, dst, sems, index, to):
        return pltpu.make_async_remote_copy(
            src_ref=src,
            dst_ref=dst,
            send_sem=sems.at[(0,) + index],
            recv_sem=sems.at[(1,) + index],
            device_id=to,
            device_id_type=pl.DeviceIdType.MESH,
        )

    right_x, left_x = (x + 1) % SIDE, (x + 3) % SIDE
    far_x = (x + 2) % SIDE
    dp_steps = [(i, j) for i in (2, 1, 3, 0) for j in (2, 1, 3, 0) if (i, j) != (0, 0)]
    enc_steps = [(i, j) for i in (4, 3, 5, 2, 6, 1, 7, 0) for j in (0, 1) if (i, j) != (0, 0)]

    load_targets = pltpu.make_async_copy(targets, own_targets, local_sem.at[0])
    load_encoded = pltpu.make_async_copy(encoded, enc_all.at[dp], local_sem.at[1])
    load_k = pltpu.make_async_copy(key_weight, weight_k, local_sem.at[2])
    load_v = pltpu.make_async_copy(value_weight, weight_v, local_sem.at[3])
    load_q = pltpu.make_async_copy(query_weight.at[:, y], weight_q.at[y], local_sem.at[4])
    load_o = pltpu.make_async_copy(
        output_weight.at[:, pl.ds(pl.multiple_of(x * 1024, 1024), 1024)],
        weight_o.at[x],
        local_sem.at[5],
    )
    load_targets.start()
    load_encoded.start()
    load_k.start()
    load_v.start()
    load_q.start()
    load_o.start()

    barrier = pltpu.get_barrier_semaphore()
    for i, j in dp_steps:
        pl.semaphore_signal(
            barrier, inc=1, device_id=device(dx=i, dy=j), device_id_type=pl.DeviceIdType.MESH
        )
    for i, j in enc_steps:
        pl.semaphore_signal(
            barrier, inc=1, device_id=device(dz=i, dc=j), device_id_type=pl.DeviceIdType.MESH
        )
    pl.semaphore_wait(barrier, len(dp_steps) + len(enc_steps))

    def enc_copy(i, j):
        return remote(
            encoded, enc_all.at[dp], enc_sem, (i * SIDE + j,), device(dx=i, dy=j)
        )

    for i, j in dp_steps:
        enc_copy(i, j).start()

    load_targets.wait()
    owners = [slot[e * TILES + i] // TILES for i in range(TILES)]

    def tile_copy(i, j):
        to = device(dz=i, dc=j)
        return to[1], remote(
            sent_tiles.at[i * 2 + j], came_tiles.at[e], tile_sem, (i * 2 + j,), to
        )

    def tile_for(peer):
        found = jnp.int32(0)
        for i in range(1, TILES):
            found = jnp.where(owners[i] == peer, i, found)
        return own_targets[found]

    for i, j in enc_steps:
        peer, copy = tile_copy(i, j)
        sent_tiles[i * 2 + j] = tile_for(peer)
        copy.start()
    came_tiles[e] = tile_for(e)

    def wq_copy(j):
        part = pl.ds(2 * c, 2)
        return remote(
            query_weight.at[part, (y + j) % SIDE],
            weight_q.at[y, part],
            wq_sem,
            (j,),
            device(dy=j),
        )

    def wo_copy(i):
        part = pl.ds(pl.multiple_of(c * TILE, TILE), TILE)
        return remote(
            output_weight.at[part, pl.ds(pl.multiple_of(((x + i) % SIDE) * 1024, 1024), 1024)],
            weight_o.at[x, part],
            wo_sem,
            (i,),
            device(dx=i),
        )

    for i in (2, 1, 3):
        wq_copy(i).start()
    for i in (2, 1, 3):
        wo_copy(i).start()

    load_encoded.wait()
    for i, j in dp_steps:
        enc_copy(i, j).wait()
    load_k.wait()
    load_v.wait()

    def project(block, sums):
        rows = enc_all[block]
        return (
            sums[0] + jnp.dot(rows, weight_k[block], preferred_element_type=F32),
            sums[1] + jnp.dot(rows, weight_v[block], preferred_element_type=F32),
        )

    zero = jnp.zeros((TILE, HD), F32)
    key_rows, value_rows = lax.fori_loop(0, ENC_PEERS, project, (zero, zero))
    kv[e, 0] = key_rows.astype(BF)
    kv[e, 1] = value_rows.astype(BF)

    def kv_block(step):
        return ((z + step + DEPTH) % DEPTH) * 2 + c

    def kv_copy(step, way):
        block = kv_block(-step * way)
        return remote(
            kv.at[block],
            kv.at[block],
            kv_sem,
            (step, 0 if way > 0 else 1),
            device(dz=way),
        )

    def kv_last(way):
        block = kv_block(-3 * way)
        part = 0 if way > 0 else 1
        return remote(
            kv.at[block, part], kv.at[block, part], kv_sem, (3, part), device(dz=way)
        )

    def kv_pair(step):
        block = kv_block(step)
        return remote(kv.at[block], kv.at[block], kvp_sem, ((step + DEPTH) % DEPTH,), device(dc=1))

    kv_copy(0, 1).start()
    kv_copy(0, -1).start()
    kv_pair(0).start()

    def wq_pair(j):
        block = (y + SIDE - j) % SIDE
        part = pl.ds(2 * c, 2)
        ref = weight_q.at[block, part]
        return remote(ref, ref, pair_sem, (j,), device(dc=1))

    def wo_pair(i):
        block = (x + SIDE - i) % SIDE
        part = pl.ds(pl.multiple_of(c * TILE, TILE), TILE)
        ref = weight_o.at[block, part]
        return remote(ref, ref, pair_sem, (SIDE + i,), device(dc=1))

    for i in (1, 3, 2):
        wq_copy(i).wait()
        wq_pair(i).start()

    for i, j in enc_steps:
        tile_copy(i, j)[1].wait()

    lanes = lax.broadcasted_iota(jnp.int32, (TILE, TILE), 1)
    eye = lax.broadcasted_iota(jnp.int32, (TILE, TILE), 0) == lanes

    def to_row(column):
        return jnp.sum(jnp.where(eye, column, 0.0), axis=0, keepdims=True)

    def to_column(row):
        return jnp.sum(jnp.where(eye, row, 0.0), axis=1, keepdims=True)

    slots = slot_row[...]
    first_lane = lax.broadcasted_iota(jnp.int32, (1, TILE), 1)
    sources = [
        jnp.max(jnp.where(slots == e * TILES + s, first_lane, 0)) for s in range(TILES)
    ]
    gain_two = gain[pl.ds(2 * dp, 2)]
    gain_row = jnp.concatenate([gain_two[0:1], gain_two[1:2]], axis=1)

    def gather_copy(buf, sems, t, way):
        ref = buf.at[t, x]
        return remote(ref, ref, sems, (t, 0 if way > 0 else 1), device(dx=way))

    for s in range(TILES):
        picked = came_tiles[sources[s] // TILES].astype(F32)
        squares[dp, s : s + 1] = to_row(jnp.sum(picked * picked, axis=1, keepdims=True))
        rows_q[s, x] = (picked * gain_row).astype(BF)
        gather_copy(rows_q, gather_q_sem, s, 1).start()
        gather_copy(rows_q, gather_q_sem, s, -1).start()

    def sq_copy(i, j):
        ref = squares.at[dp]
        return remote(ref, ref, sq_sem, (i * SIDE + j,), device(dx=i, dy=j))

    for i, j in dp_steps:
        sq_copy(i, j).start()

    for i in (1, 3, 2):
        wo_copy(i).wait()
        wo_pair(i).start()

    def pass_copy(buf, sems, t, way):
        block = left_x if way > 0 else right_x
        part = pl.ds(0 if way > 0 else HALF, HALF)
        ref = buf.at[t, block, part]
        return remote(ref, ref, sems, (t, 0 if way > 0 else 1), device(dx=way))

    def pass_on(buf, first_sems, sems, t):
        gather_copy(buf, first_sems, t, 1).wait_recv()
        pass_copy(buf, sems, t, 1).start()
        gather_copy(buf, first_sems, t, -1).wait_recv()
        pass_copy(buf, sems, t, -1).start()

    def far_copy(far, half, sems, t, way):
        part = 0 if way > 0 else 1
        return remote(
            far.at[t, pl.ds(part * HALF, HALF)], half.at[t, part], sems, (t, part), device(dy=way)
        )

    def multiply(buf, sems, weight_block, kept, far, half, far_sems, t):
        pass_copy(buf, sems, t, 1).wait_recv()
        pass_copy(buf, sems, t, -1).wait_recv()
        rows = [buf[t, i] for i in range(SIDE)]

        def block(step):
            n = (y + step) % SIDE
            total = jnp.dot(rows[0], weight_block(0, n), preferred_element_type=F32)
            for i in range(1, SIDE):
                total = total + jnp.dot(rows[i], weight_block(i, n), preferred_element_type=F32)
            return total

        far[t] = block(2).astype(BF)
        far_copy(far, half, far_sems, t, 1).start()
        far_copy(far, half, far_sems, t, -1).start()
        kept[t, 0] = block(1)
        kept[t, 1] = block(3)
        kept[t, 2] = block(0)

    def near_copy(near, total, sems, t, way):
        part = 0 if way > 0 else 1
        return remote(near.at[t, part], total.at[t, part], sems, (t, part), device(dy=way))

    def add_far(kept, far, half, far_sems, near, total, near_sems, t):
        far_copy(far, half, far_sems, t, 1).wait_recv()
        near[t, 0, :HALF] = (kept[t, 0, :HALF] + half[t, 0].astype(F32)).astype(BF)
        near[t, 0, HALF:] = kept[t, 0, HALF:].astype(BF)
        near_copy(near, total, near_sems, t, 1).start()
        far_copy(far, half, far_sems, t, -1).wait_recv()
        near[t, 1, :HALF] = kept[t, 1, :HALF].astype(BF)
        near[t, 1, HALF:] = (kept[t, 1, HALF:] + half[t, 1].astype(F32)).astype(BF)
        near_copy(near, total, near_sems, t, -1).start()

    def finish(kept, near, total, near_sems, t):
        near_copy(near, total, near_sems, t, 1).wait_recv()
        near_copy(near, total, near_sems, t, -1).wait_recv()
        return kept[t, 2] + total[t, 0].astype(F32) + total[t, 1].astype(F32)

    def wq_block(i, n):
        return weight_q[n, i]

    def wo_block(i, n):
        return weight_o[i, :, pl.ds(pl.multiple_of(n * HD, HD), HD)]

    enc_row = jnp.concatenate([encoder_segment[i : i + 1] for i in range(ENC_PEERS)], axis=1)

    def attend(t):
        total = squares[0, pl.ds(t, 1)]
        for i in range(1, SIDE * SIDE):
            total = total + squares[i, pl.ds(t, 1)]
        scale = to_column(lax.rsqrt(total * (1.0 / FEATURES) + 1e-6))
        queries = (finish(kept_q, near_q, sum_q, near_q_sem, t) * scale).astype(BF)
        source = sources[0]
        for s in range(1, TILES):
            source = jnp.where(t == s, sources[s], source)
        segment = to_column(target_segment[pl.ds(source, 1)].astype(F32)).astype(jnp.int32)
        keys = kv[:, 0].reshape(ENC_PEERS * TILE, HD)
        values = kv[:, 1].reshape(ENC_PEERS * TILE, HD)
        scores = lax.dot_general(
            queries, keys, (((1,), (1,)), ((), ())), preferred_element_type=F32
        )
        allowed = segment == enc_row
        scores = jnp.where(allowed, scores, -1e30)
        top = jnp.max(scores, axis=-1, keepdims=True)
        weights = jnp.where(allowed, jnp.exp(scores - top), 0.0)
        denominator = jnp.sum(weights, axis=-1, keepdims=True)
        summed = jnp.dot(weights.astype(BF), values, preferred_element_type=F32)
        rows_o[t, x] = (summed / denominator).astype(BF)
        gather_copy(rows_o, gather_o_sem, t, 1).start()
        gather_copy(rows_o, gather_o_sem, t, -1).start()

    def out_copy(t):
        return pltpu.make_async_copy(
            out_rows.at[t], out.at[pl.ds(pl.multiple_of(t * TILE, TILE), TILE)], out_sem.at[t]
        )

    def kv_step(h):
        kv_copy(h - 1, 1).wait_recv()
        if h < 3:
            kv_copy(h, 1).start()
        else:
            kv_last(1).start()
        kv_pair(-h).start()
        kv_copy(h - 1, -1).wait_recv()
        if h < 3:
            kv_copy(h, -1).start()
        else:
            kv_last(-1).start()
        kv_pair(h).start()

    load_q.wait()
    load_o.wait()

    def turn(t, carry):
        for h in (1, 2, 3):

            @pl.when(t == h - 1)
            def _():
                kv_step(h)

        @pl.when(t < TILES)
        def _():
            pass_on(rows_q, gather_q_sem, pass_q_sem, t)

        @pl.when(t == 1)
        def _():
            for i in (1, 3, 2):
                wq_pair(i).wait()

        @pl.when((t >= 1) & (t < TILES + 1))
        def _():
            multiply(rows_q, pass_q_sem, wq_block, kept_q, far_q, half_q, far_q_sem, t - 1)

        @pl.when((t >= 2) & (t < TILES + 2))
        def _():
            add_far(kept_q, far_q, half_q, far_q_sem, near_q, sum_q, near_q_sem, t - 2)

        @pl.when(t == 3)
        def _():
            for i, j in dp_steps:
                sq_copy(i, j).wait()
            kv_last(1).wait_recv()
            kv_last(-1).wait_recv()
            kv_pair(4).start()
            for h in range(DEPTH):
                kv_pair(h).wait_recv()

        @pl.when((t >= 3) & (t < TILES + 3))
        def _():
            attend(t - 3)

        @pl.when((t >= 4) & (t < TILES + 4))
        def _():
            pass_on(rows_o, gather_o_sem, pass_o_sem, t - 4)

        @pl.when(t == 5)
        def _():
            for i in (1, 3, 2):
                wo_pair(i).wait()

        @pl.when((t >= 5) & (t < TILES + 5))
        def _():
            multiply(rows_o, pass_o_sem, wo_block, kept_o, far_o, half_o, far_o_sem, t - 5)

        @pl.when((t >= 6) & (t < TILES + 6))
        def _():
            add_far(kept_o, far_o, half_o, far_o_sem, near_o, sum_o, near_o_sem, t - 6)

        @pl.when((t >= 7) & (t < TILES + 7))
        def _():
            out_rows[t - 7] = finish(kept_o, near_o, sum_o, near_o_sem, t - 7).astype(BF)
            out_copy(t - 7).start()

        return carry

    lax.fori_loop(0, TILES + 7, turn, 0)

    for h in range(3):
        kv_copy(h, 1).wait_send()
        kv_copy(h, -1).wait_send()
    kv_last(1).wait_send()
    kv_last(-1).wait_send()
    for h in range(DEPTH):
        kv_pair(h).wait_send()

    def drain(t, carry):
        for way in (1, -1):
            gather_copy(rows_q, gather_q_sem, t, way).wait_send()
            gather_copy(rows_o, gather_o_sem, t, way).wait_send()
            pass_copy(rows_q, pass_q_sem, t, way).wait_send()
            pass_copy(rows_o, pass_o_sem, t, way).wait_send()
            far_copy(far_q, half_q, far_q_sem, t, way).wait_send()
            far_copy(far_o, half_o, far_o_sem, t, way).wait_send()
            near_copy(near_q, sum_q, near_q_sem, t, way).wait_send()
            near_copy(near_o, sum_o, near_o_sem, t, way).wait_send()
        out_copy(t).wait()
        return carry

    lax.fori_loop(0, TILES, drain, 0)


def local(
    targets,
    encoded,
    norm_gain,
    query_weight,
    key_weight,
    value_weight,
    output_weight,
    target_segment,
    encoder_segment,
    tile_slot,
):
    any_space = pl.BlockSpec(memory_space=pl.ANY)
    vmem = pl.BlockSpec(memory_space=pltpu.VMEM)
    smem = pl.BlockSpec(memory_space=pltpu.SMEM)
    sem = pltpu.SemaphoreType.DMA
    tile = (TILE, HD)
    scratch = [
        pltpu.VMEM((TILES,) + tile, BF),
        pltpu.VMEM((ENC_PEERS,) + tile, BF),
        pltpu.VMEM((ENC_PEERS,) + tile, BF),
        pltpu.VMEM((ENC_PEERS,) + tile, BF),
        pltpu.VMEM((ENC_PEERS, HD, HD), BF),
        pltpu.VMEM((ENC_PEERS, HD, HD), BF),
        pltpu.VMEM((SIDE, SIDE, HD, HD), BF),
        pltpu.VMEM((SIDE, HD, SIDE * HD), BF),
        pltpu.VMEM((ENC_PEERS, 2) + tile, BF),
        pltpu.VMEM((SIDE * SIDE, TILES, TILE), F32),
        pltpu.VMEM((TILES, SIDE) + tile, BF),
        pltpu.VMEM((TILES, SIDE) + tile, BF),
        pltpu.VMEM((TILES, 3) + tile, F32),
        pltpu.VMEM((TILES, 3) + tile, F32),
        pltpu.VMEM((TILES,) + tile, BF),
        pltpu.VMEM((TILES,) + tile, BF),
        pltpu.VMEM((TILES, 2, HALF, HD), BF),
        pltpu.VMEM((TILES, 2, HALF, HD), BF),
        pltpu.VMEM((TILES, 2) + tile, BF),
        pltpu.VMEM((TILES, 2) + tile, BF),
        pltpu.VMEM((TILES, 2) + tile, BF),
        pltpu.VMEM((TILES, 2) + tile, BF),
        pltpu.VMEM((TILES,) + tile, BF),
        sem((6,)),
        sem((2, SIDE * SIDE)),
        sem((2, ENC_PEERS)),
        sem((2, SIDE)),
        sem((2, SIDE)),
        sem((2, 2 * SIDE)),
        sem((2, 4, 2)),
        sem((2, DEPTH)),
        sem((2, SIDE * SIDE)),
        sem((2, TILES, 2)),
        sem((2, TILES, 2)),
        sem((2, TILES, 2)),
        sem((2, TILES, 2)),
        sem((2, TILES, 2)),
        sem((2, TILES, 2)),
        sem((2, TILES, 2)),
        sem((2, TILES, 2)),
        sem((TILES,)),
    ]
    return pl.pallas_call(
        kernel,
        out_shape=jax.ShapeDtypeStruct((TILES * TILE, HD), BF),
        in_specs=[any_space] * 2 + [vmem] + [any_space] * 4 + [vmem] * 3 + [smem],
        out_specs=any_space,
        scratch_shapes=scratch,
        compiler_params=pltpu.CompilerParams(
            collective_id=0, has_side_effects=True, vmem_limit_bytes=56 << 20
        ),
        cost_estimate=pl.CostEstimate(
            flops=7_000_000_000, bytes_accessed=10_000_000, transcendentals=2_000_000
        ),
        name="cross_attention",
    )(
        targets.reshape((TILES,) + tile),
        encoded,
        norm_gain.reshape(2 * SIDE * SIDE, TILE),
        query_weight.reshape(SIDE, SIDE, HD, HD),
        key_weight.reshape(ENC_PEERS, HD, HD),
        value_weight.reshape(ENC_PEERS, HD, HD),
        output_weight,
        target_segment.reshape(-1, TILE),
        encoder_segment.reshape(-1, TILE),
        tile_slot.reshape(1, -1),
        tile_slot,
    )


def solution(mesh):
    return jax.shard_map(
        local,
        mesh=mesh,
        in_specs=(
            P("enc", "dp"),
            P("enc", "dp"),
            P(),
            P(None, "dp"),
            P(None, "dp"),
            P(None, "dp"),
            P("dp", None),
            P(),
            P(),
            P(),
        ),
        out_specs=P("enc", "dp"),
        check_vma=False,
    )
```

```python
import jax
import jax.numpy as jnp
from jax import lax
from jax.experimental import pallas as pl
from jax.experimental.pallas import tpu as pltpu
from jax.sharding import PartitionSpec as P

HD = 256
TILE = 128
TILES = 8
HALF = TILE // 2
SIDE = 4
DEPTH = 8
ENC_PEERS = 16
AHEAD = 3
LAG = 2
FEATURES = 4096
BF = jnp.bfloat16
F32 = jnp.float32


def kernel(
    targets,
    encoded,
    gain,
    query_weight,
    key_weight,
    value_weight,
    output_weight,
    target_segment,
    encoder_segment,
    slot_row,
    slot,
    out,
    own_targets,
    sent_tiles,
    came_tiles,
    enc_all,
    weight_k,
    weight_v,
    weight_q,
    weight_o,
    kv,
    squares,
    rows_q,
    rows_o,
    kept_q,
    kept_o,
    far_q,
    far_o,
    half_q,
    half_o,
    near_q,
    near_o,
    sum_q,
    sum_o,
    out_rows,
    local_sem,
    enc_sem,
    tile_sem,
    wq_sem,
    wo_sem,
    pair_sem,
    kv_sem,
    kvp_sem,
    sq_sem,
    gather_q_sem,
    gather_o_sem,
    pass_q_sem,
    pass_o_sem,
    far_q_sem,
    far_o_sem,
    near_q_sem,
    near_o_sem,
    out_sem,
):
    dp = lax.axis_index("dp")
    e = lax.axis_index("enc")
    x, y = dp // SIDE, dp % SIDE
    z, c = e // 2, e % 2

    def device(dx=0, dy=0, dz=0, dc=0):
        return (
            ((x + dx + SIDE) % SIDE) * SIDE + (y + dy + SIDE) % SIDE,
            ((z + dz + DEPTH) % DEPTH) * 2 + (c + dc) % 2,
        )

    def remote(src, dst, sems, index, to):
        return pltpu.make_async_remote_copy(
            src_ref=src,
            dst_ref=dst,
            send_sem=sems.at[(0,) + index],
            recv_sem=sems.at[(1,) + index],
            device_id=to,
            device_id_type=pl.DeviceIdType.MESH,
        )

    right_x, left_x = (x + 1) % SIDE, (x + 3) % SIDE
    far_x = (x + 2) % SIDE
    dp_steps = [(i, j) for i in (2, 1, 3, 0) for j in (2, 1, 3, 0) if (i, j) != (0, 0)]
    enc_steps = [(i, j) for i in (4, 3, 5, 2, 6, 1, 7, 0) for j in (0, 1) if (i, j) != (0, 0)]

    load_targets = pltpu.make_async_copy(targets, own_targets, local_sem.at[0])
    load_encoded = pltpu.make_async_copy(encoded, enc_all.at[dp], local_sem.at[1])
    load_k = pltpu.make_async_copy(key_weight, weight_k, local_sem.at[2])
    load_v = pltpu.make_async_copy(value_weight, weight_v, local_sem.at[3])
    load_q = pltpu.make_async_copy(query_weight.at[:, y], weight_q.at[y], local_sem.at[4])
    load_o = pltpu.make_async_copy(
        output_weight.at[:, pl.ds(pl.multiple_of(x * 1024, 1024), 1024)],
        weight_o.at[x],
        local_sem.at[5],
    )
    load_targets.start()
    load_encoded.start()
    load_k.start()
    load_v.start()
    load_q.start()
    load_o.start()

    barrier = pltpu.get_barrier_semaphore()
    for i, j in dp_steps:
        pl.semaphore_signal(
            barrier, inc=1, device_id=device(dx=i, dy=j), device_id_type=pl.DeviceIdType.MESH
        )
    for i, j in enc_steps:
        pl.semaphore_signal(
            barrier, inc=1, device_id=device(dz=i, dc=j), device_id_type=pl.DeviceIdType.MESH
        )
    load_targets.wait()
    owners = [slot[e * TILES + i] // TILES for i in range(TILES)]

    def tile_copy(i, j):
        to = device(dz=i, dc=j)
        return remote(
            sent_tiles.at[i * 2 + j], came_tiles.at[e], tile_sem, (i * 2 + j,), to
        )

    def tile_for(peer):
        found = jnp.int32(0)
        for i in range(1, TILES):
            found = jnp.where(owners[i] == peer, i, found)
        return own_targets[found]

    for i, j in enc_steps:
        sent_tiles[i * 2 + j] = tile_for(device(dz=i, dc=j)[1])
    came_tiles[e] = tile_for(e)

    pl.semaphore_wait(barrier, len(dp_steps) + len(enc_steps))
    for i, j in enc_steps:
        tile_copy(i, j).start()

    def enc_copy(i, j):
        return remote(
            encoded, enc_all.at[dp], enc_sem, (i * SIDE + j,), device(dx=i, dy=j)
        )

    for i, j in dp_steps:
        enc_copy(i, j).start()

    def wq_copy(j):
        part = pl.ds(2 * c, 2)
        return remote(
            query_weight.at[part, (y + j) % SIDE],
            weight_q.at[y, part],
            wq_sem,
            (j,),
            device(dy=j),
        )

    def wo_copy(i):
        part = pl.ds(pl.multiple_of(c * TILE, TILE), TILE)
        return remote(
            output_weight.at[part, pl.ds(pl.multiple_of(((x + i) % SIDE) * 1024, 1024), 1024)],
            weight_o.at[x, part],
            wo_sem,
            (i,),
            device(dx=i),
        )

    load_encoded.wait()
    for i, j in dp_steps:
        enc_copy(i, j).wait()
    for i in (2, 1, 3):
        wq_copy(i).start()
    for i in (2, 1, 3):
        wo_copy(i).start()
    load_k.wait()
    load_v.wait()

    def project(block, sums):
        rows = enc_all[block]
        return (
            sums[0] + jnp.dot(rows, weight_k[block], preferred_element_type=F32),
            sums[1] + jnp.dot(rows, weight_v[block], preferred_element_type=F32),
        )

    zero = jnp.zeros((TILE, HD), F32)
    key_rows, value_rows = lax.fori_loop(0, ENC_PEERS, project, (zero, zero))
    kv[e, 0] = key_rows.astype(BF)
    kv[e, 1] = value_rows.astype(BF)

    def kv_block(step):
        return ((z + step + DEPTH) % DEPTH) * 2 + c

    def kv_copy(step, way):
        block = kv_block(-step * way)
        return remote(
            kv.at[block],
            kv.at[block],
            kv_sem,
            (step, 0 if way > 0 else 1),
            device(dz=way),
        )

    def kv_last(way):
        block = kv_block(-3 * way)
        part = 0 if way > 0 else 1
        return remote(
            kv.at[block, part], kv.at[block, part], kv_sem, (3, part), device(dz=way)
        )

    def kv_pair(step):
        block = kv_block(step)
        return remote(kv.at[block], kv.at[block], kvp_sem, ((step + DEPTH) % DEPTH,), device(dc=1))

    kv_copy(0, 1).start()
    kv_copy(0, -1).start()
    kv_pair(0).start()

    def wq_pair(j):
        block = (y + SIDE - j) % SIDE
        part = pl.ds(2 * c, 2)
        ref = weight_q.at[block, part]
        return remote(ref, ref, pair_sem, (j,), device(dc=1))

    def wo_pair(i):
        block = (x + SIDE - i) % SIDE
        part = pl.ds(pl.multiple_of(c * TILE, TILE), TILE)
        ref = weight_o.at[block, part]
        return remote(ref, ref, pair_sem, (SIDE + i,), device(dc=1))

    for i in (1, 3, 2):
        wq_copy(i).wait()
        wq_pair(i).start()

    for i, j in enc_steps:
        tile_copy(i, j).wait()

    lanes = lax.broadcasted_iota(jnp.int32, (TILE, TILE), 1)
    eye = lax.broadcasted_iota(jnp.int32, (TILE, TILE), 0) == lanes

    def to_row(column):
        return jnp.sum(jnp.where(eye, column, 0.0), axis=0, keepdims=True)

    def to_column(row):
        return jnp.sum(jnp.where(eye, row, 0.0), axis=1, keepdims=True)

    slots = slot_row[...]
    first_lane = lax.broadcasted_iota(jnp.int32, (1, TILE), 1)
    sources = [
        jnp.max(jnp.where(slots == e * TILES + s, first_lane, 0)) for s in range(TILES)
    ]
    gain_two = gain[pl.ds(2 * dp, 2)]
    gain_row = jnp.concatenate([gain_two[0:1], gain_two[1:2]], axis=1)

    def gather_copy(buf, sems, t, way):
        ref = buf.at[t, x]
        return remote(ref, ref, sems, (t, 0 if way > 0 else 1), device(dx=way))

    for s in range(TILES):
        picked = came_tiles[sources[s] // TILES].astype(F32)
        squares[dp, s : s + 1] = to_row(jnp.sum(picked * picked, axis=1, keepdims=True))
        rows_q[s, x] = (picked * gain_row).astype(BF)
        if s < AHEAD:
            gather_copy(rows_q, gather_q_sem, s, 1).start()
            gather_copy(rows_q, gather_q_sem, s, -1).start()

    def sq_copy(i, j):
        ref = squares.at[dp]
        return remote(ref, ref, sq_sem, (i * SIDE + j,), device(dx=i, dy=j))

    for i, j in dp_steps:
        sq_copy(i, j).start()

    for i in (1, 3, 2):
        wo_copy(i).wait()
        wo_pair(i).start()

    def pass_copy(buf, sems, t, way):
        block = left_x if way > 0 else right_x
        part = pl.ds(0 if way > 0 else HALF, HALF)
        ref = buf.at[t, block, part]
        return remote(ref, ref, sems, (t, 0 if way > 0 else 1), device(dx=way))

    def pass_on(buf, first_sems, sems, t):
        gather_copy(buf, first_sems, t, 1).wait_recv()
        pass_copy(buf, sems, t, 1).start()
        gather_copy(buf, first_sems, t, -1).wait_recv()
        pass_copy(buf, sems, t, -1).start()

    def far_copy(far, half, sems, t, way):
        part = 0 if way > 0 else 1
        return remote(
            far.at[t, pl.ds(part * HALF, HALF)], half.at[t, part], sems, (t, part), device(dy=way)
        )

    def multiply(buf, sems, weight_block, kept, far, half, far_sems, t):
        pass_copy(buf, sems, t, 1).wait_recv()
        pass_copy(buf, sems, t, -1).wait_recv()
        rows = [buf[t, i] for i in range(SIDE)]

        def block(step):
            n = (y + step) % SIDE
            total = jnp.dot(rows[0], weight_block(0, n), preferred_element_type=F32)
            for i in range(1, SIDE):
                total = total + jnp.dot(rows[i], weight_block(i, n), preferred_element_type=F32)
            return total

        far[t] = block(2).astype(BF)
        far_copy(far, half, far_sems, t, 1).start()
        far_copy(far, half, far_sems, t, -1).start()
        kept[t, 0] = block(1)
        kept[t, 1] = block(3)
        kept[t, 2] = block(0)

    def near_copy(near, total, sems, t, way):
        part = 0 if way > 0 else 1
        return remote(near.at[t, part], total.at[t, part], sems, (t, part), device(dy=way))

    def add_far(kept, far, half, far_sems, near, total, near_sems, t):
        far_copy(far, half, far_sems, t, 1).wait_recv()
        near[t, 0, :HALF] = (kept[t, 0, :HALF] + half[t, 0].astype(F32)).astype(BF)
        near[t, 0, HALF:] = kept[t, 0, HALF:].astype(BF)
        near_copy(near, total, near_sems, t, 1).start()
        far_copy(far, half, far_sems, t, -1).wait_recv()
        near[t, 1, :HALF] = kept[t, 1, :HALF].astype(BF)
        near[t, 1, HALF:] = (kept[t, 1, HALF:] + half[t, 1].astype(F32)).astype(BF)
        near_copy(near, total, near_sems, t, -1).start()

    def finish(kept, near, total, near_sems, t):
        near_copy(near, total, near_sems, t, 1).wait_recv()
        near_copy(near, total, near_sems, t, -1).wait_recv()
        return kept[t, 2] + total[t, 0].astype(F32) + total[t, 1].astype(F32)

    def wq_block(i, n):
        return weight_q[n, i]

    def wo_block(i, n):
        return weight_o[i, :, pl.ds(pl.multiple_of(n * HD, HD), HD)]

    enc_row = jnp.concatenate([encoder_segment[i : i + 1] for i in range(ENC_PEERS)], axis=1)

    def attend(t):
        total = squares[0, pl.ds(t, 1)]
        for i in range(1, SIDE * SIDE):
            total = total + squares[i, pl.ds(t, 1)]
        scale = to_column(lax.rsqrt(total * (1.0 / FEATURES) + 1e-6))
        queries = (finish(kept_q, near_q, sum_q, near_q_sem, t) * scale).astype(BF)
        source = sources[0]
        for s in range(1, TILES):
            source = jnp.where(t == s, sources[s], source)
        segment = to_column(target_segment[pl.ds(source, 1)].astype(F32)).astype(jnp.int32)
        keys = kv[:, 0].reshape(ENC_PEERS * TILE, HD)
        values = kv[:, 1].reshape(ENC_PEERS * TILE, HD)
        scores = lax.dot_general(
            queries, keys, (((1,), (1,)), ((), ())), preferred_element_type=F32
        )
        allowed = segment == enc_row
        scores = jnp.where(allowed, scores, -1e30)
        top = jnp.max(scores, axis=-1, keepdims=True)
        weights = jnp.where(allowed, jnp.exp(scores - top), 0.0)
        denominator = jnp.sum(weights, axis=-1, keepdims=True)
        summed = jnp.dot(weights.astype(BF), values, preferred_element_type=F32)
        rows_o[t, x] = (summed / denominator).astype(BF)
        gather_copy(rows_o, gather_o_sem, t, 1).start()
        gather_copy(rows_o, gather_o_sem, t, -1).start()

    def out_copy(t):
        return pltpu.make_async_copy(
            out_rows.at[t], out.at[pl.ds(pl.multiple_of(t * TILE, TILE), TILE)], out_sem.at[t]
        )

    def kv_step(h):
        kv_copy(h - 1, 1).wait_recv()
        if h < 3:
            kv_copy(h, 1).start()
        else:
            kv_last(1).start()
        kv_pair(-h).start()
        kv_copy(h - 1, -1).wait_recv()
        if h < 3:
            kv_copy(h, -1).start()
        else:
            kv_last(-1).start()
        kv_pair(h).start()

    load_q.wait()
    load_o.wait()

    def turn(t, carry):
        def stage(number, body):
            tile = t - number * LAG

            @pl.when((tile >= 0) & (tile < TILES))
            def _():
                body(tile)

        def once(at, body):
            pl.when(t == at)(body)

        def wait_wq():
            for i in (1, 3, 2):
                wq_pair(i).wait()

        def wait_wo():
            for i in (1, 3, 2):
                wo_pair(i).wait()

        def last_kv():
            kv_last(1).wait_recv()
            kv_last(-1).wait_recv()
            kv_pair(4).start()

        def wait_kv():
            for i, j in dp_steps:
                sq_copy(i, j).wait()
            for h in range(DEPTH):
                kv_pair(h).wait_recv()

        def next_gather():
            gather_copy(rows_q, gather_q_sem, t + AHEAD, 1).start()
            gather_copy(rows_q, gather_q_sem, t + AHEAD, -1).start()

        def write(tile):
            out_rows[tile] = finish(kept_o, near_o, sum_o, near_o_sem, tile).astype(BF)
            out_copy(tile).start()

        stage(0, lambda i: pass_on(rows_q, gather_q_sem, pass_q_sem, i))
        pl.when(t < TILES - AHEAD)(next_gather)
        once(LAG, wait_wq)
        stage(1, lambda i: multiply(rows_q, pass_q_sem, wq_block, kept_q, far_q, half_q, far_q_sem, i))
        stage(2, lambda i: add_far(kept_q, far_q, half_q, far_q_sem, near_q, sum_q, near_q_sem, i))
        once(1, lambda: kv_step(2))
        once(3, lambda: kv_step(3))
        once(5, last_kv)
        once(3 * LAG, wait_kv)
        stage(3, attend)
        stage(4, lambda i: pass_on(rows_o, gather_o_sem, pass_o_sem, i))
        once(5 * LAG, wait_wo)
        stage(5, lambda i: multiply(rows_o, pass_o_sem, wo_block, kept_o, far_o, half_o, far_o_sem, i))
        stage(6, lambda i: add_far(kept_o, far_o, half_o, far_o_sem, near_o, sum_o, near_o_sem, i))
        stage(7, write)
        return carry

    kv_step(1)
    lax.fori_loop(0, TILES + 7 * LAG, turn, 0)

    for h in range(3):
        kv_copy(h, 1).wait_send()
        kv_copy(h, -1).wait_send()
    kv_last(1).wait_send()
    kv_last(-1).wait_send()
    for h in range(DEPTH):
        kv_pair(h).wait_send()

    def drain(t, carry):
        for way in (1, -1):
            gather_copy(rows_q, gather_q_sem, t, way).wait_send()
            gather_copy(rows_o, gather_o_sem, t, way).wait_send()
            pass_copy(rows_q, pass_q_sem, t, way).wait_send()
            pass_copy(rows_o, pass_o_sem, t, way).wait_send()
            far_copy(far_q, half_q, far_q_sem, t, way).wait_send()
            far_copy(far_o, half_o, far_o_sem, t, way).wait_send()
            near_copy(near_q, sum_q, near_q_sem, t, way).wait_send()
            near_copy(near_o, sum_o, near_o_sem, t, way).wait_send()
        out_copy(t).wait()
        return carry

    lax.fori_loop(0, TILES, drain, 0)


def local(
    targets,
    encoded,
    norm_gain,
    query_weight,
    key_weight,
    value_weight,
    output_weight,
    target_segment,
    encoder_segment,
    tile_slot,
):
    any_space = pl.BlockSpec(memory_space=pl.ANY)
    vmem = pl.BlockSpec(memory_space=pltpu.VMEM)
    smem = pl.BlockSpec(memory_space=pltpu.SMEM)
    sem = pltpu.SemaphoreType.DMA
    tile = (TILE, HD)
    scratch = [
        pltpu.VMEM((TILES,) + tile, BF),
        pltpu.VMEM((ENC_PEERS,) + tile, BF),
        pltpu.VMEM((ENC_PEERS,) + tile, BF),
        pltpu.VMEM((ENC_PEERS,) + tile, BF),
        pltpu.VMEM((ENC_PEERS, HD, HD), BF),
        pltpu.VMEM((ENC_PEERS, HD, HD), BF),
        pltpu.VMEM((SIDE, SIDE, HD, HD), BF),
        pltpu.VMEM((SIDE, HD, SIDE * HD), BF),
        pltpu.VMEM((ENC_PEERS, 2) + tile, BF),
        pltpu.VMEM((SIDE * SIDE, TILES, TILE), F32),
        pltpu.VMEM((TILES, SIDE) + tile, BF),
        pltpu.VMEM((TILES, SIDE) + tile, BF),
        pltpu.VMEM((TILES, 3) + tile, F32),
        pltpu.VMEM((TILES, 3) + tile, F32),
        pltpu.VMEM((TILES,) + tile, BF),
        pltpu.VMEM((TILES,) + tile, BF),
        pltpu.VMEM((TILES, 2, HALF, HD), BF),
        pltpu.VMEM((TILES, 2, HALF, HD), BF),
        pltpu.VMEM((TILES, 2) + tile, BF),
        pltpu.VMEM((TILES, 2) + tile, BF),
        pltpu.VMEM((TILES, 2) + tile, BF),
        pltpu.VMEM((TILES, 2) + tile, BF),
        pltpu.VMEM((TILES,) + tile, BF),
        sem((6,)),
        sem((2, SIDE * SIDE)),
        sem((2, ENC_PEERS)),
        sem((2, SIDE)),
        sem((2, SIDE)),
        sem((2, 2 * SIDE)),
        sem((2, 4, 2)),
        sem((2, DEPTH)),
        sem((2, SIDE * SIDE)),
        sem((2, TILES, 2)),
        sem((2, TILES, 2)),
        sem((2, TILES, 2)),
        sem((2, TILES, 2)),
        sem((2, TILES, 2)),
        sem((2, TILES, 2)),
        sem((2, TILES, 2)),
        sem((2, TILES, 2)),
        sem((TILES,)),
    ]
    return pl.pallas_call(
        kernel,
        out_shape=jax.ShapeDtypeStruct((TILES * TILE, HD), BF),
        in_specs=[any_space] * 2 + [vmem] + [any_space] * 4 + [vmem] * 3 + [smem],
        out_specs=any_space,
        scratch_shapes=scratch,
        compiler_params=pltpu.CompilerParams(
            collective_id=0, has_side_effects=True, vmem_limit_bytes=56 << 20
        ),
        cost_estimate=pl.CostEstimate(
            flops=7_000_000_000, bytes_accessed=10_000_000, transcendentals=2_000_000
        ),
        name="cross_attention",
    )(
        targets.reshape((TILES,) + tile),
        encoded,
        norm_gain.reshape(2 * SIDE * SIDE, TILE),
        query_weight.reshape(SIDE, SIDE, HD, HD),
        key_weight.reshape(ENC_PEERS, HD, HD),
        value_weight.reshape(ENC_PEERS, HD, HD),
        output_weight,
        target_segment.reshape(-1, TILE),
        encoder_segment.reshape(-1, TILE),
        tile_slot.reshape(1, -1),
        tile_slot,
    )


def solution(mesh):
    return jax.shard_map(
        local,
        mesh=mesh,
        in_specs=(
            P("enc", "dp"),
            P("enc", "dp"),
            P(),
            P(None, "dp"),
            P(None, "dp"),
            P(None, "dp"),
            P("dp", None),
            P(),
            P(),
            P(),
        ),
        out_specs=P("enc", "dp"),
        check_vma=False,
    )
```

```python
import jax
import jax.numpy as jnp
from jax import lax
from jax.experimental import pallas as pl
from jax.experimental.pallas import tpu as pltpu
from jax.sharding import PartitionSpec as P

HD = 256
TILE = 128
TILES = 8
HALF = TILE // 2
SIDE = 4
DEPTH = 8
ENC_PEERS = 16
BATCH = 4
GROUP = 5
FEATURES = 4096
BF = jnp.bfloat16
F32 = jnp.float32


def kernel(
    targets,
    encoded,
    gain,
    query_weight,
    key_weight,
    value_weight,
    output_weight,
    target_segment,
    encoder_segment,
    slot_row,
    slot,
    out,
    own_targets,
    sent_tiles,
    came_tiles,
    enc_all,
    weight_k,
    weight_v,
    weight_q,
    weight_o,
    kv,
    squares,
    rows_q,
    rows_o,
    kept_q,
    kept_o,
    far_q,
    far_o,
    half_q,
    half_o,
    near_q,
    near_o,
    sum_q,
    sum_o,
    out_rows,
    out_tiles,
    kv_total,
    local_sem,
    enc_sem,
    tile_sem,
    wq_sem,
    wo_sem,
    pair_sem,
    kv_sem,
    kvp_sem,
    sq_sem,
    gather_q_sem,
    gather_o_sem,
    pass_q_sem,
    pass_o_sem,
    far_q_sem,
    far_o_sem,
    near_q_sem,
    near_o_sem,
    out_sem,
):
    dp = lax.axis_index("dp")
    e = lax.axis_index("enc")
    x, y = dp // SIDE, dp % SIDE
    z, c = e // 2, e % 2

    def device(dx=0, dy=0, dz=0, dc=0):
        return (
            ((x + dx + SIDE) % SIDE) * SIDE + (y + dy + SIDE) % SIDE,
            ((z + dz + DEPTH) % DEPTH) * 2 + (c + dc) % 2,
        )

    def remote(src, dst, sems, index, to):
        return pltpu.make_async_remote_copy(
            src_ref=src,
            dst_ref=dst,
            send_sem=sems.at[(0,) + index],
            recv_sem=sems.at[(1,) + index],
            device_id=to,
            device_id_type=pl.DeviceIdType.MESH,
        )

    right_x, left_x = (x + 1) % SIDE, (x + 3) % SIDE
    far_x = (x + 2) % SIDE
    dp_steps = [(i, j) for i in (2, 1, 3, 0) for j in (2, 1, 3, 0) if (i, j) != (0, 0)]
    enc_steps = [(i, j) for i in (0, 1, 7, 2, 6, 3, 5, 4) for j in (0, 1)][1:]

    load_targets = pltpu.make_async_copy(targets, own_targets, local_sem.at[0])
    load_encoded = pltpu.make_async_copy(encoded, enc_all.at[dp], local_sem.at[1])
    load_k = pltpu.make_async_copy(key_weight, weight_k, local_sem.at[2])
    load_v = pltpu.make_async_copy(value_weight, weight_v, local_sem.at[3])
    load_q = pltpu.make_async_copy(query_weight.at[:, y], weight_q.at[y], local_sem.at[4])
    load_o = pltpu.make_async_copy(
        output_weight.at[:, pl.ds(pl.multiple_of(x * 1024, 1024), 1024)],
        weight_o.at[x],
        local_sem.at[5],
    )
    load_targets.start()
    load_encoded.start()
    load_k.start()
    load_v.start()
    load_q.start()
    load_o.start()

    barrier = pltpu.get_barrier_semaphore()
    for i, j in dp_steps:
        pl.semaphore_signal(
            barrier, inc=1, device_id=device(dx=i, dy=j), device_id_type=pl.DeviceIdType.MESH
        )
    for i, j in enc_steps:
        pl.semaphore_signal(
            barrier, inc=1, device_id=device(dz=i, dc=j), device_id_type=pl.DeviceIdType.MESH
        )
    load_targets.wait()
    owners = [slot[e * TILES + i] // TILES for i in range(TILES)]

    def tile_copy(rank):
        i, j = enc_steps[rank - 1]
        return remote(
            sent_tiles.at[rank], came_tiles.at[rank], tile_sem, (rank,), device(dz=i, dc=j)
        )

    def tile_for(peer):
        found = jnp.int32(0)
        for i in range(1, TILES):
            found = jnp.where(owners[i] == peer, i, found)
        return own_targets[found]

    for rank in range(1, ENC_PEERS):
        i, j = enc_steps[rank - 1]
        sent_tiles[rank] = tile_for(device(dz=i, dc=j)[1])
    came_tiles[0] = tile_for(e)

    pl.semaphore_wait(barrier, len(dp_steps) + len(enc_steps))
    for rank in range(1, ENC_PEERS):
        tile_copy(rank).start()

    def enc_copy(i, j):
        return remote(
            encoded, enc_all.at[dp], enc_sem, (i * SIDE + j,), device(dx=i, dy=j)
        )

    for i, j in dp_steps:
        enc_copy(i, j).start()

    def wq_copy(j):
        part = pl.ds(2 * c, 2)
        return remote(
            query_weight.at[part, (y + j) % SIDE],
            weight_q.at[y, part],
            wq_sem,
            (j,),
            device(dy=j),
        )

    def wo_copy(i):
        part = pl.ds(pl.multiple_of(c * TILE, TILE), TILE)
        return remote(
            output_weight.at[part, pl.ds(pl.multiple_of(((x + i) % SIDE) * 1024, 1024), 1024)],
            weight_o.at[x, part],
            wo_sem,
            (i,),
            device(dx=i),
        )

    load_k.wait()
    load_v.wait()
    load_encoded.wait()

    def project(block):
        rows = enc_all[block]
        return (
            jnp.dot(rows, weight_k[block], preferred_element_type=F32),
            jnp.dot(rows, weight_v[block], preferred_element_type=F32),
        )

    def add_blocks(blocks):
        key_part, value_part = project(blocks[0])
        for block in blocks[1:]:
            more = project(block)
            key_part, value_part = key_part + more[0], value_part + more[1]
        return key_part, value_part

    kv_total[0], kv_total[1] = add_blocks([dp])
    for first in range(0, len(dp_steps), GROUP):
        group = dp_steps[first : first + GROUP]
        for i, j in group:
            enc_copy(i, j).wait_recv()
        if first == 0:
            for i in (2, 1, 3):
                wq_copy(i).start()
            for i in (2, 1, 3):
                wo_copy(i).start()
        parts = add_blocks([device(dx=-i, dy=-j)[0] for i, j in group])
        kv_total[0] += parts[0]
        kv_total[1] += parts[1]
    kv[e, 0] = kv_total[0].astype(BF)
    kv[e, 1] = kv_total[1].astype(BF)

    def kv_block(step):
        return ((z + step + DEPTH) % DEPTH) * 2 + c

    def kv_copy(step, way):
        block = kv_block(-step * way)
        return remote(
            kv.at[block],
            kv.at[block],
            kv_sem,
            (step, 0 if way > 0 else 1),
            device(dz=way),
        )

    def kv_last(way):
        block = kv_block(-3 * way)
        part = 0 if way > 0 else 1
        return remote(
            kv.at[block, part], kv.at[block, part], kv_sem, (3, part), device(dz=way)
        )

    def kv_pair(step):
        block = kv_block(step)
        return remote(kv.at[block], kv.at[block], kvp_sem, ((step + DEPTH) % DEPTH,), device(dc=1))

    kv_copy(0, 1).start()
    kv_copy(0, -1).start()
    kv_pair(0).start()

    def wq_pair(j):
        block = (y + SIDE - j) % SIDE
        part = pl.ds(2 * c, 2)
        ref = weight_q.at[block, part]
        return remote(ref, ref, pair_sem, (j,), device(dc=1))

    def wo_pair(i):
        block = (x + SIDE - i) % SIDE
        part = pl.ds(pl.multiple_of(c * TILE, TILE), TILE)
        ref = weight_o.at[block, part]
        return remote(ref, ref, pair_sem, (SIDE + i,), device(dc=1))

    lanes = lax.broadcasted_iota(jnp.int32, (TILE, TILE), 1)
    eye = lax.broadcasted_iota(jnp.int32, (TILE, TILE), 0) == lanes

    def to_row(column):
        return jnp.sum(jnp.where(eye, column, 0.0), axis=0, keepdims=True)

    def to_column(row):
        return jnp.sum(jnp.where(eye, row, 0.0), axis=1, keepdims=True)

    slots = slot_row[...]
    first_lane = lax.broadcasted_iota(jnp.int32, (1, TILE), 1)
    slot_sources = [
        jnp.max(jnp.where(slots == e * TILES + s, first_lane, 0)) for s in range(TILES)
    ]

    def rank_of(source):
        home = source // TILES
        gap = (z - home // 2 + DEPTH) % DEPTH
        place = jnp.where(gap <= DEPTH // 2, jnp.maximum(2 * gap - 1, 0), 2 * (DEPTH - gap))
        return 2 * place + jnp.where(home % 2 == c, 0, 1)

    ranks = [rank_of(source) for source in slot_sources]
    places = []
    for s in range(TILES):
        place = jnp.int32(0)
        for other in range(TILES):
            if other != s:
                place = place + jnp.where(ranks[other] < ranks[s], 1, 0)
        places.append(place)

    def of_tile(values, t):
        value = jnp.int32(0)
        for s in range(TILES):
            value = jnp.where(places[s] == t, values[s], value)
        return value

    gain_two = gain[pl.ds(2 * dp, 2)]
    gain_row = jnp.concatenate([gain_two[0:1], gain_two[1:2]], axis=1)

    def gather_copy(buf, sems, t, way):
        ref = buf.at[t, x]
        return remote(ref, ref, sems, (t, 0 if way > 0 else 1), device(dx=way))

    def pick(t):
        rank = of_tile(ranks, t)
        picked = came_tiles[t]
        for more in range(1, TILES + 1):
            picked = jnp.where(rank == t + more, came_tiles[t + more], picked)
        picked = picked.astype(F32)
        rows_q[t, x] = (picked * gain_row).astype(BF)
        gather_copy(rows_q, gather_q_sem, t, 1).start()
        gather_copy(rows_q, gather_q_sem, t, -1).start()
        squares[t // BATCH, dp, pl.ds(t % BATCH, 1)] = to_row(
            jnp.sum(picked * picked, axis=1, keepdims=True)
        )

    def sq_copy(batch, i, j):
        ref = squares.at[batch, dp]
        return remote(ref, ref, sq_sem, (batch, i * SIDE + j), device(dx=i, dy=j))

    def pass_copy(buf, sems, t, way):
        block = left_x if way > 0 else right_x
        part = pl.ds(0 if way > 0 else HALF, HALF)
        ref = buf.at[t, block, part]
        return remote(ref, ref, sems, (t, 0 if way > 0 else 1), device(dx=way))

    def pass_on(buf, first_sems, sems, t):
        gather_copy(buf, first_sems, t, 1).wait_recv()
        pass_copy(buf, sems, t, 1).start()
        gather_copy(buf, first_sems, t, -1).wait_recv()
        pass_copy(buf, sems, t, -1).start()

    def far_copy(far, half, sems, t, way):
        part = 0 if way > 0 else 1
        return remote(
            far.at[t, pl.ds(part * HALF, HALF)], half.at[t, part], sems, (t, part), device(dy=way)
        )

    def multiply(buf, sems, weight_block, kept, far, half, far_sems, t):
        pass_copy(buf, sems, t, 1).wait_recv()
        pass_copy(buf, sems, t, -1).wait_recv()
        rows = [buf[t, i] for i in range(SIDE)]

        def block(step):
            n = (y + step) % SIDE
            total = jnp.dot(rows[0], weight_block(0, n), preferred_element_type=F32)
            for i in range(1, SIDE):
                total = total + jnp.dot(rows[i], weight_block(i, n), preferred_element_type=F32)
            return total

        far[t] = block(2).astype(BF)
        far_copy(far, half, far_sems, t, 1).start()
        far_copy(far, half, far_sems, t, -1).start()
        kept[t, 0] = block(1)
        kept[t, 1] = block(3)
        kept[t, 2] = block(0)

    def near_copy(near, total, sems, t, way):
        part = 0 if way > 0 else 1
        return remote(near.at[t, part], total.at[t, part], sems, (t, part), device(dy=way))

    def add_far(kept, far, half, far_sems, near, total, near_sems, t):
        far_copy(far, half, far_sems, t, 1).wait_recv()
        near[t, 0, :HALF] = (kept[t, 0, :HALF] + half[t, 0].astype(F32)).astype(BF)
        near[t, 0, HALF:] = kept[t, 0, HALF:].astype(BF)
        near_copy(near, total, near_sems, t, 1).start()
        far_copy(far, half, far_sems, t, -1).wait_recv()
        near[t, 1, :HALF] = kept[t, 1, :HALF].astype(BF)
        near[t, 1, HALF:] = (kept[t, 1, HALF:] + half[t, 1].astype(F32)).astype(BF)
        near_copy(near, total, near_sems, t, -1).start()

    def finish(kept, near, total, near_sems, t):
        near_copy(near, total, near_sems, t, 1).wait_recv()
        near_copy(near, total, near_sems, t, -1).wait_recv()
        return kept[t, 2] + total[t, 0].astype(F32) + total[t, 1].astype(F32)

    def wq_block(i, n):
        return weight_q[n, i]

    def wo_block(i, n):
        return weight_o[i, :, pl.ds(pl.multiple_of(n * HD, HD), HD)]

    enc_row = jnp.concatenate([encoder_segment[i : i + 1] for i in range(ENC_PEERS)], axis=1)

    def attend(t):
        batch, row = t // BATCH, pl.ds(t % BATCH, 1)
        total = squares[batch, 0, row]
        for i in range(1, SIDE * SIDE):
            total = total + squares[batch, i, row]
        scale = to_column(lax.rsqrt(total * (1.0 / FEATURES) + 1e-6))
        queries = (finish(kept_q, near_q, sum_q, near_q_sem, t) * scale).astype(BF)
        segment = to_column(target_segment[pl.ds(of_tile(slot_sources, t), 1)].astype(F32)).astype(jnp.int32)
        keys = kv[:, 0].reshape(ENC_PEERS * TILE, HD)
        values = kv[:, 1].reshape(ENC_PEERS * TILE, HD)
        scores = lax.dot_general(
            queries, keys, (((1,), (1,)), ((), ())), preferred_element_type=F32
        )
        allowed = segment == enc_row
        scores = jnp.where(allowed, scores, -1e30)
        top = jnp.max(scores, axis=-1, keepdims=True)
        weights = jnp.where(allowed, jnp.exp(scores - top), 0.0)
        denominator = jnp.sum(weights, axis=-1, keepdims=True)
        summed = jnp.dot(weights.astype(BF), values, preferred_element_type=F32)
        rows_o[t, x] = (summed / denominator).astype(BF)
        gather_copy(rows_o, gather_o_sem, t, 1).start()
        gather_copy(rows_o, gather_o_sem, t, -1).start()

    def out_copy(t):
        return pltpu.make_async_copy(
            out_tiles.at[t], out.at[pl.ds(pl.multiple_of(t * TILE, TILE), TILE)], out_sem.at[t]
        )

    def kv_step(h):
        kv_copy(h - 1, 1).wait_recv()
        if h < 3:
            kv_copy(h, 1).start()
        else:
            kv_last(1).start()
        kv_pair(-h).start()
        kv_copy(h - 1, -1).wait_recv()
        if h < 3:
            kv_copy(h, -1).start()
        else:
            kv_last(-1).start()
        kv_pair(h).start()

    load_q.wait()
    load_o.wait()

    def turn(t, carry):
        def stage(late, body):
            tile = t - late

            @pl.when((tile >= 0) & (tile < TILES))
            def _():
                body(tile)

        def once(at, body):
            pl.when(t == at)(body)

        def pass_wq():
            for i in (1, 3, 2):
                wq_copy(i).wait()
                wq_pair(i).start()

        def pass_wo():
            for i in (1, 3, 2):
                wo_copy(i).wait()
                wo_pair(i).start()

        def wait_wq():
            for i in (1, 3, 2):
                wq_pair(i).wait()

        def wait_wo():
            for i in (1, 3, 2):
                wo_pair(i).wait()

        def last_kv():
            kv_last(1).wait_recv()
            kv_last(-1).wait_recv()
            kv_pair(4).start()

        def wait_kv():
            for h in range(DEPTH):
                kv_pair(h).wait_recv()

        def send_squares(batch):
            for i, j in dp_steps:
                sq_copy(batch, i, j).start()

        def wait_squares(batch):
            for i, j in dp_steps:
                sq_copy(batch, i, j).wait()

        def write(tile):
            out_rows[tile] = finish(kept_o, near_o, sum_o, near_o_sem, tile).astype(BF)

        for tile in range(1, TILES):
            once(tile, tile_copy(TILES + tile).wait_recv)
        stage(0, pick)
        for batch in (0, 1):
            once((batch + 1) * BATCH - 1, lambda batch=batch: send_squares(batch))
        once(1, lambda: kv_step(1))
        once(2, pass_wq)
        stage(2, lambda i: pass_on(rows_q, gather_q_sem, pass_q_sem, i))
        once(3, lambda: kv_step(2))
        stage(5, lambda i: add_far(kept_q, far_q, half_q, far_q_sem, near_q, sum_q, near_q_sem, i))
        once(5, lambda: kv_step(3))
        once(7, last_kv)
        once(7, wait_kv)
        for batch in (0, 1):
            once(7 + batch * BATCH, lambda batch=batch: wait_squares(batch))
        stage(7, attend)
        once(6, pass_wo)
        stage(9, lambda i: pass_on(rows_o, gather_o_sem, pass_o_sem, i))
        stage(12, lambda i: add_far(kept_o, far_o, half_o, far_o_sem, near_o, sum_o, near_o_sem, i))
        stage(14, write)
        once(3, wait_wq)
        stage(3, lambda i: multiply(rows_q, pass_q_sem, wq_block, kept_q, far_q, half_q, far_q_sem, i))
        once(10, wait_wo)
        stage(10, lambda i: multiply(rows_o, pass_o_sem, wo_block, kept_o, far_o, half_o, far_o_sem, i))
        return carry

    for rank in range(1, TILES + 1):
        tile_copy(rank).wait_recv()
    lax.fori_loop(0, TILES + 14, turn, 0)

    for s in range(TILES):
        out_tiles[s] = out_rows[places[s]]
        out_copy(s).start()

    for rank in range(1, ENC_PEERS):
        tile_copy(rank).wait_send()
    for i, j in dp_steps:
        enc_copy(i, j).wait_send()
    for h in range(3):
        kv_copy(h, 1).wait_send()
        kv_copy(h, -1).wait_send()
    kv_last(1).wait_send()
    kv_last(-1).wait_send()
    for h in range(DEPTH):
        kv_pair(h).wait_send()

    def drain(t, carry):
        for way in (1, -1):
            gather_copy(rows_q, gather_q_sem, t, way).wait_send()
            gather_copy(rows_o, gather_o_sem, t, way).wait_send()
            pass_copy(rows_q, pass_q_sem, t, way).wait_send()
            pass_copy(rows_o, pass_o_sem, t, way).wait_send()
            far_copy(far_q, half_q, far_q_sem, t, way).wait_send()
            far_copy(far_o, half_o, far_o_sem, t, way).wait_send()
            near_copy(near_q, sum_q, near_q_sem, t, way).wait_send()
            near_copy(near_o, sum_o, near_o_sem, t, way).wait_send()
        out_copy(t).wait()
        return carry

    lax.fori_loop(0, TILES, drain, 0)


def local(
    targets,
    encoded,
    norm_gain,
    query_weight,
    key_weight,
    value_weight,
    output_weight,
    target_segment,
    encoder_segment,
    tile_slot,
):
    any_space = pl.BlockSpec(memory_space=pl.ANY)
    vmem = pl.BlockSpec(memory_space=pltpu.VMEM)
    smem = pl.BlockSpec(memory_space=pltpu.SMEM)
    sem = pltpu.SemaphoreType.DMA
    tile = (TILE, HD)
    scratch = [
        pltpu.VMEM((TILES,) + tile, BF),
        pltpu.VMEM((ENC_PEERS,) + tile, BF),
        pltpu.VMEM((ENC_PEERS,) + tile, BF),
        pltpu.VMEM((ENC_PEERS,) + tile, BF),
        pltpu.VMEM((ENC_PEERS, HD, HD), BF),
        pltpu.VMEM((ENC_PEERS, HD, HD), BF),
        pltpu.VMEM((SIDE, SIDE, HD, HD), BF),
        pltpu.VMEM((SIDE, HD, SIDE * HD), BF),
        pltpu.VMEM((ENC_PEERS, 2) + tile, BF),
        pltpu.VMEM((2, SIDE * SIDE, TILES, TILE), F32),
        pltpu.VMEM((TILES, SIDE) + tile, BF),
        pltpu.VMEM((TILES, SIDE) + tile, BF),
        pltpu.VMEM((TILES, 3) + tile, F32),
        pltpu.VMEM((TILES, 3) + tile, F32),
        pltpu.VMEM((TILES,) + tile, BF),
        pltpu.VMEM((TILES,) + tile, BF),
        pltpu.VMEM((TILES, 2, HALF, HD), BF),
        pltpu.VMEM((TILES, 2, HALF, HD), BF),
        pltpu.VMEM((TILES, 2) + tile, BF),
        pltpu.VMEM((TILES, 2) + tile, BF),
        pltpu.VMEM((TILES, 2) + tile, BF),
        pltpu.VMEM((TILES, 2) + tile, BF),
        pltpu.VMEM((TILES,) + tile, BF),
        pltpu.VMEM((TILES,) + tile, BF),
        pltpu.VMEM((2,) + tile, F32),
        sem((6,)),
        sem((2, SIDE * SIDE)),
        sem((2, ENC_PEERS)),
        sem((2, SIDE)),
        sem((2, SIDE)),
        sem((2, 2 * SIDE)),
        sem((2, 4, 2)),
        sem((2, DEPTH)),
        sem((2, 2, SIDE * SIDE)),
        sem((2, TILES, 2)),
        sem((2, TILES, 2)),
        sem((2, TILES, 2)),
        sem((2, TILES, 2)),
        sem((2, TILES, 2)),
        sem((2, TILES, 2)),
        sem((2, TILES, 2)),
        sem((2, TILES, 2)),
        sem((TILES,)),
    ]
    return pl.pallas_call(
        kernel,
        out_shape=jax.ShapeDtypeStruct((TILES * TILE, HD), BF),
        in_specs=[any_space] * 2 + [vmem] + [any_space] * 4 + [vmem] * 3 + [smem],
        out_specs=any_space,
        scratch_shapes=scratch,
        compiler_params=pltpu.CompilerParams(
            collective_id=0, has_side_effects=True, vmem_limit_bytes=56 << 20
        ),
        cost_estimate=pl.CostEstimate(
            flops=7_000_000_000, bytes_accessed=10_000_000, transcendentals=2_000_000
        ),
        name="cross_attention",
    )(
        targets.reshape((TILES,) + tile),
        encoded,
        norm_gain.reshape(2 * SIDE * SIDE, TILE),
        query_weight.reshape(SIDE, SIDE, HD, HD),
        key_weight.reshape(ENC_PEERS, HD, HD),
        value_weight.reshape(ENC_PEERS, HD, HD),
        output_weight,
        target_segment.reshape(-1, TILE),
        encoder_segment.reshape(-1, TILE),
        tile_slot.reshape(1, -1),
        tile_slot,
    )


def solution(mesh):
    return jax.shard_map(
        local,
        mesh=mesh,
        in_specs=(
            P("enc", "dp"),
            P("enc", "dp"),
            P(),
            P(None, "dp"),
            P(None, "dp"),
            P(None, "dp"),
            P("dp", None),
            P(),
            P(),
            P(),
        ),
        out_specs=P("enc", "dp"),
        check_vma=False,
    )
```

```python
import jax
import jax.numpy as jnp
from jax import lax
from jax.experimental import pallas as pl
from jax.experimental.pallas import tpu as pltpu
from jax.sharding import PartitionSpec as P

HD = 256
TILE = 128
TILES = 8
HALF = TILE // 2
SIDE = 4
DEPTH = 8
ENC_PEERS = 16
BATCH = 4
NEAR = 10
FEATURES = 4096
BF = jnp.bfloat16
F32 = jnp.float32


def kernel(
    targets,
    encoded,
    gain,
    query_weight,
    key_weight,
    value_weight,
    output_weight,
    target_segment,
    encoder_segment,
    slot_row,
    slot,
    out,
    own_targets,
    sent_tiles,
    came_tiles,
    enc_all,
    weight_k,
    weight_v,
    weight_q,
    weight_o,
    kv,
    squares,
    rows_q,
    rows_o,
    kept_q,
    kept_o,
    far_q,
    far_o,
    half_q,
    half_o,
    near_q,
    near_o,
    sum_q,
    sum_o,
    out_rows,
    out_tiles,
    local_sem,
    enc_sem,
    tile_sem,
    wq_sem,
    wo_sem,
    pair_sem,
    kv_sem,
    kvp_sem,
    sq_sem,
    gather_q_sem,
    gather_o_sem,
    pass_q_sem,
    pass_o_sem,
    far_q_sem,
    far_o_sem,
    near_q_sem,
    near_o_sem,
    out_sem,
):
    dp = lax.axis_index("dp")
    e = lax.axis_index("enc")
    x, y = dp // SIDE, dp % SIDE
    z, c = e // 2, e % 2

    def device(dx=0, dy=0, dz=0, dc=0):
        return (
            ((x + dx + SIDE) % SIDE) * SIDE + (y + dy + SIDE) % SIDE,
            ((z + dz + DEPTH) % DEPTH) * 2 + (c + dc) % 2,
        )

    def remote(src, dst, sems, index, to):
        return pltpu.make_async_remote_copy(
            src_ref=src,
            dst_ref=dst,
            send_sem=sems.at[(0,) + index],
            recv_sem=sems.at[(1,) + index],
            device_id=to,
            device_id_type=pl.DeviceIdType.MESH,
        )

    right_x, left_x = (x + 1) % SIDE, (x + 3) % SIDE
    far_x = (x + 2) % SIDE
    dp_steps = [(i, j) for i in (2, 1, 3, 0) for j in (2, 1, 3, 0) if (i, j) != (0, 0)]
    enc_steps = [(i, j) for i in (0, 1, 7, 2, 6, 3, 5, 4) for j in (0, 1)][1:]

    load_targets = pltpu.make_async_copy(targets, own_targets, local_sem.at[0])
    load_encoded = pltpu.make_async_copy(encoded, enc_all.at[x, y], local_sem.at[1])
    load_k = pltpu.make_async_copy(key_weight, weight_k, local_sem.at[2])
    load_v = pltpu.make_async_copy(value_weight, weight_v, local_sem.at[3])
    load_q = pltpu.make_async_copy(query_weight.at[:, y], weight_q.at[y], local_sem.at[4])
    load_o = pltpu.make_async_copy(
        output_weight.at[:, pl.ds(pl.multiple_of(x * 1024, 1024), 1024)],
        weight_o.at[x],
        local_sem.at[5],
    )
    load_targets.start()
    load_encoded.start()
    load_k.start()
    load_v.start()
    load_q.start()
    load_o.start()

    barrier = pltpu.get_barrier_semaphore()
    for i, j in dp_steps:
        pl.semaphore_signal(
            barrier, inc=1, device_id=device(dx=i, dy=j), device_id_type=pl.DeviceIdType.MESH
        )
    for i, j in enc_steps:
        pl.semaphore_signal(
            barrier, inc=1, device_id=device(dz=i, dc=j), device_id_type=pl.DeviceIdType.MESH
        )
    load_targets.wait()
    owners = [slot[e * TILES + i] // TILES for i in range(TILES)]

    def tile_copy(rank):
        i, j = enc_steps[rank - 1]
        return remote(
            sent_tiles.at[rank], came_tiles.at[rank], tile_sem, (rank,), device(dz=i, dc=j)
        )

    def tile_for(peer):
        found = jnp.int32(0)
        for i in range(1, TILES):
            found = jnp.where(owners[i] == peer, i, found)
        return own_targets[found]

    for rank in range(1, ENC_PEERS):
        i, j = enc_steps[rank - 1]
        sent_tiles[rank] = tile_for(device(dz=i, dc=j)[1])
    came_tiles[0] = tile_for(e)

    pl.semaphore_wait(barrier, len(dp_steps) + len(enc_steps))
    for rank in range(1, NEAR):
        tile_copy(rank).start()

    upper, lower = pl.ds(0, HALF), pl.ds(HALF, HALF)

    def enc_first(i):
        return (
            remote(
                encoded.at[upper], enc_all.at[x, y, upper], enc_sem, (0, i), device(dx=i)
            ),
            remote(
                encoded.at[lower], enc_all.at[x, y, lower], enc_sem, (1, i), device(dy=i)
            ),
        )

    def enc_second(i):
        column, line = enc_all.at[:, y, upper], enc_all.at[x, :, lower]
        return (
            remote(column, column, enc_sem, (2, i), device(dy=i)),
            remote(line, line, enc_sem, (3, i), device(dx=i)),
        )

    for i in (2, 1, 3):
        for copy in enc_first(i):
            copy.start()

    def wq_copy(j):
        part = pl.ds(2 * c, 2)
        return remote(
            query_weight.at[part, (y + j) % SIDE],
            weight_q.at[y, part],
            wq_sem,
            (j,),
            device(dy=j),
        )

    def wo_copy(i):
        part = pl.ds(pl.multiple_of(c * TILE, TILE), TILE)
        return remote(
            output_weight.at[part, pl.ds(pl.multiple_of(((x + i) % SIDE) * 1024, 1024), 1024)],
            weight_o.at[x, part],
            wo_sem,
            (i,),
            device(dx=i),
        )

    load_encoded.wait()
    for i in (1, 3, 2):
        for copy in enc_first(i):
            copy.wait_recv()
    for i in (2, 1, 3):
        for copy in enc_second(i):
            copy.start()
    for i in (2, 1, 3):
        wq_copy(i).start()
        wo_copy(i).start()

    load_k.wait()
    load_v.wait()
    for i in (1, 3, 2):
        for copy in enc_second(i):
            copy.wait_recv()

    def project(weight):
        total = jnp.zeros((TILE, HD), F32)
        for i in range(SIDE):
            part = jnp.zeros((TILE, HD), F32)
            for j in range(SIDE):
                part = part + jnp.dot(
                    enc_all[i, j], weight[i * SIDE + j], preferred_element_type=F32
                )
            total = total + part
        return total.astype(BF)

    kv[e, 0] = project(weight_k)
    kv[e, 1] = project(weight_v)

    def kv_block(step):
        return ((z + step + DEPTH) % DEPTH) * 2 + c

    def kv_copy(step, way):
        block = kv_block(-step * way)
        return remote(
            kv.at[block],
            kv.at[block],
            kv_sem,
            (step, 0 if way > 0 else 1),
            device(dz=way),
        )

    def kv_last(way):
        block = kv_block(-3 * way)
        part = 0 if way > 0 else 1
        return remote(
            kv.at[block, part], kv.at[block, part], kv_sem, (3, part), device(dz=way)
        )

    def kv_pair(step):
        block = kv_block(step)
        return remote(kv.at[block], kv.at[block], kvp_sem, ((step + DEPTH) % DEPTH,), device(dc=1))

    kv_copy(0, 1).start()
    kv_copy(0, -1).start()
    kv_pair(0).start()
    for rank in (10, 12):
        tile_copy(rank).start()

    def wq_pair(j):
        block = (y + SIDE - j) % SIDE
        part = pl.ds(2 * c, 2)
        ref = weight_q.at[block, part]
        return remote(ref, ref, pair_sem, (j,), device(dc=1))

    def wo_pair(i):
        block = (x + SIDE - i) % SIDE
        part = pl.ds(pl.multiple_of(c * TILE, TILE), TILE)
        ref = weight_o.at[block, part]
        return remote(ref, ref, pair_sem, (SIDE + i,), device(dc=1))

    lanes = lax.broadcasted_iota(jnp.int32, (TILE, TILE), 1)
    eye = lax.broadcasted_iota(jnp.int32, (TILE, TILE), 0) == lanes

    def to_row(column):
        return jnp.sum(jnp.where(eye, column, 0.0), axis=0, keepdims=True)

    def to_column(row):
        return jnp.sum(jnp.where(eye, row, 0.0), axis=1, keepdims=True)

    slots = slot_row[...]
    first_lane = lax.broadcasted_iota(jnp.int32, (1, TILE), 1)
    slot_sources = [
        jnp.max(jnp.where(slots == e * TILES + s, first_lane, 0)) for s in range(TILES)
    ]

    def rank_of(source):
        home = source // TILES
        gap = (z - home // 2 + DEPTH) % DEPTH
        place = jnp.where(gap <= DEPTH // 2, jnp.maximum(2 * gap - 1, 0), 2 * (DEPTH - gap))
        return 2 * place + jnp.where(home % 2 == c, 0, 1)

    ranks = [rank_of(source) for source in slot_sources]
    places = []
    for s in range(TILES):
        place = jnp.int32(0)
        for other in range(TILES):
            if other != s:
                place = place + jnp.where(ranks[other] < ranks[s], 1, 0)
        places.append(place)

    def of_tile(values, t):
        value = jnp.int32(0)
        for s in range(TILES):
            value = jnp.where(places[s] == t, values[s], value)
        return value

    gain_two = gain[pl.ds(2 * dp, 2)]
    gain_row = jnp.concatenate([gain_two[0:1], gain_two[1:2]], axis=1)

    def gather_copy(buf, sems, t, way):
        ref = buf.at[t, x]
        return remote(ref, ref, sems, (t, 0 if way > 0 else 1), device(dx=way))

    def pick(t):
        rank = of_tile(ranks, t)
        picked = came_tiles[t]
        for more in range(1, TILES + 1):
            picked = jnp.where(rank == t + more, came_tiles[t + more], picked)
        picked = picked.astype(F32)
        rows_q[t, x] = (picked * gain_row).astype(BF)
        gather_copy(rows_q, gather_q_sem, t, 1).start()
        gather_copy(rows_q, gather_q_sem, t, -1).start()
        squares[t // BATCH, dp, pl.ds(t % BATCH, 1)] = to_row(
            jnp.sum(picked * picked, axis=1, keepdims=True)
        )

    def sq_copy(batch, i, j):
        ref = squares.at[batch, dp]
        return remote(ref, ref, sq_sem, (batch, i * SIDE + j), device(dx=i, dy=j))

    def pass_copy(buf, sems, t, way):
        block = left_x if way > 0 else right_x
        part = pl.ds(0 if way > 0 else HALF, HALF)
        ref = buf.at[t, block, part]
        return remote(ref, ref, sems, (t, 0 if way > 0 else 1), device(dx=way))

    def pass_on(buf, first_sems, sems, t):
        gather_copy(buf, first_sems, t, 1).wait_recv()
        pass_copy(buf, sems, t, 1).start()
        gather_copy(buf, first_sems, t, -1).wait_recv()
        pass_copy(buf, sems, t, -1).start()

    def far_copy(far, half, sems, t, way):
        part = 0 if way > 0 else 1
        return remote(
            far.at[t, pl.ds(part * HALF, HALF)], half.at[t, part], sems, (t, part), device(dy=way)
        )

    def multiply(buf, sems, weight_block, kept, far, half, far_sems, t):
        pass_copy(buf, sems, t, 1).wait_recv()
        pass_copy(buf, sems, t, -1).wait_recv()
        rows = [buf[t, i] for i in range(SIDE)]

        def block(step):
            n = (y + step) % SIDE
            total = jnp.dot(rows[0], weight_block(0, n), preferred_element_type=F32)
            for i in range(1, SIDE):
                total = total + jnp.dot(rows[i], weight_block(i, n), preferred_element_type=F32)
            return total

        far[t] = block(2).astype(BF)
        far_copy(far, half, far_sems, t, 1).start()
        far_copy(far, half, far_sems, t, -1).start()
        kept[t, 0] = block(1)
        kept[t, 1] = block(3)
        kept[t, 2] = block(0)

    def near_copy(near, total, sems, t, way):
        part = 0 if way > 0 else 1
        return remote(near.at[t, part], total.at[t, part], sems, (t, part), device(dy=way))

    def add_far(kept, far, half, far_sems, near, total, near_sems, t):
        far_copy(far, half, far_sems, t, 1).wait_recv()
        near[t, 0, :HALF] = (kept[t, 0, :HALF] + half[t, 0].astype(F32)).astype(BF)
        near[t, 0, HALF:] = kept[t, 0, HALF:].astype(BF)
        near_copy(near, total, near_sems, t, 1).start()
        far_copy(far, half, far_sems, t, -1).wait_recv()
        near[t, 1, :HALF] = kept[t, 1, :HALF].astype(BF)
        near[t, 1, HALF:] = (kept[t, 1, HALF:] + half[t, 1].astype(F32)).astype(BF)
        near_copy(near, total, near_sems, t, -1).start()

    def finish(kept, near, total, near_sems, t):
        near_copy(near, total, near_sems, t, 1).wait_recv()
        near_copy(near, total, near_sems, t, -1).wait_recv()
        return kept[t, 2] + total[t, 0].astype(F32) + total[t, 1].astype(F32)

    def wq_block(i, n):
        return weight_q[n, i]

    def wo_block(i, n):
        return weight_o[i, :, pl.ds(pl.multiple_of(n * HD, HD), HD)]

    enc_row = jnp.concatenate([encoder_segment[i : i + 1] for i in range(ENC_PEERS)], axis=1)

    def attend(t):
        batch, row = t // BATCH, pl.ds(t % BATCH, 1)
        total = squares[batch, 0, row]
        for i in range(1, SIDE * SIDE):
            total = total + squares[batch, i, row]
        scale = to_column(lax.rsqrt(total * (1.0 / FEATURES) + 1e-6))
        queries = (finish(kept_q, near_q, sum_q, near_q_sem, t) * scale).astype(BF)
        segment = to_column(target_segment[pl.ds(of_tile(slot_sources, t), 1)].astype(F32)).astype(jnp.int32)
        keys = kv[:, 0].reshape(ENC_PEERS * TILE, HD)
        values = kv[:, 1].reshape(ENC_PEERS * TILE, HD)
        scores = lax.dot_general(
            queries, keys, (((1,), (1,)), ((), ())), preferred_element_type=F32
        )
        allowed = segment == enc_row
        scores = jnp.where(allowed, scores, -1e30)
        top = jnp.max(scores, axis=-1, keepdims=True)
        weights = jnp.where(allowed, jnp.exp(scores - top), 0.0)
        denominator = jnp.sum(weights, axis=-1, keepdims=True)
        summed = jnp.dot(weights.astype(BF), values, preferred_element_type=F32)
        rows_o[t, x] = (summed / denominator).astype(BF)
        gather_copy(rows_o, gather_o_sem, t, 1).start()
        gather_copy(rows_o, gather_o_sem, t, -1).start()

    def out_copy(t):
        return pltpu.make_async_copy(
            out_tiles.at[t], out.at[pl.ds(pl.multiple_of(t * TILE, TILE), TILE)], out_sem.at[t]
        )

    def kv_step(h, far_ranks):
        kv_copy(h - 1, 1).wait_recv()
        if h < 3:
            kv_copy(h, 1).start()
        else:
            kv_last(1).start()
        kv_pair(-h).start()
        kv_copy(h - 1, -1).wait_recv()
        if h < 3:
            kv_copy(h, -1).start()
        else:
            kv_last(-1).start()
        kv_pair(h).start()
        for rank in far_ranks:
            tile_copy(rank).start()

    load_q.wait()
    load_o.wait()

    def turn(t, carry):
        def stage(late, body):
            tile = t - late

            @pl.when((tile >= 0) & (tile < TILES))
            def _():
                body(tile)

        def once(at, body):
            pl.when(t == at)(body)

        def pass_wq():
            for i in (1, 3, 2):
                wq_copy(i).wait()
                wq_pair(i).start()

        def pass_wo():
            for i in (1, 3, 2):
                wo_copy(i).wait()
                wo_pair(i).start()

        def wait_wq():
            for i in (1, 3, 2):
                wq_pair(i).wait()

        def wait_wo():
            for i in (1, 3, 2):
                wo_pair(i).wait()

        def last_kv():
            kv_last(1).wait_recv()
            kv_last(-1).wait_recv()
            kv_pair(4).start()

        def wait_kv():
            for h in range(DEPTH):
                kv_pair(h).wait_recv()

        def send_squares(batch):
            for i, j in dp_steps:
                sq_copy(batch, i, j).start()

        def wait_squares(batch):
            for i, j in dp_steps:
                sq_copy(batch, i, j).wait()

        def write(tile):
            out_rows[tile] = finish(kept_o, near_o, sum_o, near_o_sem, tile).astype(BF)

        for tile in range(1, TILES):
            once(tile, tile_copy(TILES + tile).wait_recv)
        stage(0, pick)
        for batch in (0, 1):
            once((batch + 1) * BATCH - 1, lambda batch=batch: send_squares(batch))
        once(1, lambda: kv_step(1, (11, 13)))
        once(2, pass_wq)
        stage(2, lambda i: pass_on(rows_q, gather_q_sem, pass_q_sem, i))
        once(3, lambda: kv_step(2, (14, 15)))
        stage(5, lambda i: add_far(kept_q, far_q, half_q, far_q_sem, near_q, sum_q, near_q_sem, i))
        once(5, lambda: kv_step(3, ()))
        once(7, last_kv)
        once(8, wait_kv)
        for batch in (0, 1):
            once(8 + batch * BATCH, lambda batch=batch: wait_squares(batch))
        stage(8, attend)
        once(6, pass_wo)
        stage(10, lambda i: pass_on(rows_o, gather_o_sem, pass_o_sem, i))
        stage(13, lambda i: add_far(kept_o, far_o, half_o, far_o_sem, near_o, sum_o, near_o_sem, i))
        stage(15, write)
        once(3, wait_wq)
        stage(3, lambda i: multiply(rows_q, pass_q_sem, wq_block, kept_q, far_q, half_q, far_q_sem, i))
        once(11, wait_wo)
        stage(11, lambda i: multiply(rows_o, pass_o_sem, wo_block, kept_o, far_o, half_o, far_o_sem, i))
        return carry

    for rank in range(1, TILES + 1):
        tile_copy(rank).wait_recv()
    lax.fori_loop(0, TILES + 15, turn, 0)

    for s in range(TILES):
        out_tiles[s] = out_rows[places[s]]
        out_copy(s).start()

    for rank in range(1, ENC_PEERS):
        tile_copy(rank).wait_send()
    for i in (1, 2, 3):
        for copy in enc_first(i) + enc_second(i):
            copy.wait_send()
    for h in range(3):
        kv_copy(h, 1).wait_send()
        kv_copy(h, -1).wait_send()
    kv_last(1).wait_send()
    kv_last(-1).wait_send()
    for h in range(DEPTH):
        kv_pair(h).wait_send()

    def drain(t, carry):
        for way in (1, -1):
            gather_copy(rows_q, gather_q_sem, t, way).wait_send()
            gather_copy(rows_o, gather_o_sem, t, way).wait_send()
            pass_copy(rows_q, pass_q_sem, t, way).wait_send()
            pass_copy(rows_o, pass_o_sem, t, way).wait_send()
            far_copy(far_q, half_q, far_q_sem, t, way).wait_send()
            far_copy(far_o, half_o, far_o_sem, t, way).wait_send()
            near_copy(near_q, sum_q, near_q_sem, t, way).wait_send()
            near_copy(near_o, sum_o, near_o_sem, t, way).wait_send()
        out_copy(t).wait()
        return carry

    lax.fori_loop(0, TILES, drain, 0)


def local(
    targets,
    encoded,
    norm_gain,
    query_weight,
    key_weight,
    value_weight,
    output_weight,
    target_segment,
    encoder_segment,
    tile_slot,
):
    any_space = pl.BlockSpec(memory_space=pl.ANY)
    vmem = pl.BlockSpec(memory_space=pltpu.VMEM)
    smem = pl.BlockSpec(memory_space=pltpu.SMEM)
    sem = pltpu.SemaphoreType.DMA
    tile = (TILE, HD)
    scratch = [
        pltpu.VMEM((TILES,) + tile, BF),
        pltpu.VMEM((ENC_PEERS,) + tile, BF),
        pltpu.VMEM((ENC_PEERS,) + tile, BF),
        pltpu.VMEM((SIDE, SIDE) + tile, BF),
        pltpu.VMEM((ENC_PEERS, HD, HD), BF),
        pltpu.VMEM((ENC_PEERS, HD, HD), BF),
        pltpu.VMEM((SIDE, SIDE, HD, HD), BF),
        pltpu.VMEM((SIDE, HD, SIDE * HD), BF),
        pltpu.VMEM((ENC_PEERS, 2) + tile, BF),
        pltpu.VMEM((2, SIDE * SIDE, TILES, TILE), F32),
        pltpu.VMEM((TILES, SIDE) + tile, BF),
        pltpu.VMEM((TILES, SIDE) + tile, BF),
        pltpu.VMEM((TILES, 3) + tile, F32),
        pltpu.VMEM((TILES, 3) + tile, F32),
        pltpu.VMEM((TILES,) + tile, BF),
        pltpu.VMEM((TILES,) + tile, BF),
        pltpu.VMEM((TILES, 2, HALF, HD), BF),
        pltpu.VMEM((TILES, 2, HALF, HD), BF),
        pltpu.VMEM((TILES, 2) + tile, BF),
        pltpu.VMEM((TILES, 2) + tile, BF),
        pltpu.VMEM((TILES, 2) + tile, BF),
        pltpu.VMEM((TILES, 2) + tile, BF),
        pltpu.VMEM((TILES,) + tile, BF),
        pltpu.VMEM((TILES,) + tile, BF),
        sem((6,)),
        sem((2, 4, SIDE)),
        sem((2, ENC_PEERS)),
        sem((2, SIDE)),
        sem((2, SIDE)),
        sem((2, 2 * SIDE)),
        sem((2, 4, 2)),
        sem((2, DEPTH)),
        sem((2, 2, SIDE * SIDE)),
        sem((2, TILES, 2)),
        sem((2, TILES, 2)),
        sem((2, TILES, 2)),
        sem((2, TILES, 2)),
        sem((2, TILES, 2)),
        sem((2, TILES, 2)),
        sem((2, TILES, 2)),
        sem((2, TILES, 2)),
        sem((TILES,)),
    ]
    return pl.pallas_call(
        kernel,
        out_shape=jax.ShapeDtypeStruct((TILES * TILE, HD), BF),
        in_specs=[any_space] * 2 + [vmem] + [any_space] * 4 + [vmem] * 3 + [smem],
        out_specs=any_space,
        scratch_shapes=scratch,
        compiler_params=pltpu.CompilerParams(
            collective_id=0, has_side_effects=True, vmem_limit_bytes=56 << 20
        ),
        cost_estimate=pl.CostEstimate(
            flops=7_000_000_000, bytes_accessed=10_000_000, transcendentals=2_000_000
        ),
        name="cross_attention",
    )(
        targets.reshape((TILES,) + tile),
        encoded,
        norm_gain.reshape(2 * SIDE * SIDE, TILE),
        query_weight.reshape(SIDE, SIDE, HD, HD),
        key_weight.reshape(ENC_PEERS, HD, HD),
        value_weight.reshape(ENC_PEERS, HD, HD),
        output_weight,
        target_segment.reshape(-1, TILE),
        encoder_segment.reshape(-1, TILE),
        tile_slot.reshape(1, -1),
        tile_slot,
    )


def solution(mesh):
    return jax.shard_map(
        local,
        mesh=mesh,
        in_specs=(
            P("enc", "dp"),
            P("enc", "dp"),
            P(),
            P(None, "dp"),
            P(None, "dp"),
            P(None, "dp"),
            P("dp", None),
            P(),
            P(),
            P(),
        ),
        out_specs=P("enc", "dp"),
        check_vma=False,
    )
```

```python
import jax
import jax.numpy as jnp
from jax import lax
from jax.experimental import pallas as pl
from jax.experimental.pallas import tpu as pltpu
from jax.sharding import PartitionSpec as P

HD = 256
TILE = 128
TILES = 8
HALF = TILE // 2
SIDE = 4
DEPTH = 8
ENC_PEERS = 16
BATCH = 8
NEAR = 10
SPLIT = 32
ATTEND = 8
FEATURES = 4096
BF = jnp.bfloat16
F32 = jnp.float32


def kernel(
    targets,
    encoded,
    gain,
    query_weight,
    key_weight,
    value_weight,
    output_weight,
    target_segment,
    encoder_segment,
    slot_row,
    slot,
    out,
    own_targets,
    sent_tiles,
    came_tiles,
    enc_all,
    weight_k,
    weight_v,
    weight_q,
    weight_o,
    kv,
    squares,
    rows_q,
    rows_o,
    kept_q,
    kept_o,
    far_q,
    far_o,
    half_q,
    half_o,
    near_q,
    near_o,
    sum_q,
    sum_o,
    out_rows,
    out_tiles,
    local_sem,
    enc_sem,
    tile_sem,
    wq_sem,
    wo_sem,
    pair_sem,
    kv_sem,
    kvp_sem,
    sq_sem,
    gather_q_sem,
    gather_o_sem,
    pass_q_sem,
    pass_o_sem,
    far_q_sem,
    far_o_sem,
    near_q_sem,
    near_o_sem,
    out_sem,
):
    dp = lax.axis_index("dp")
    e = lax.axis_index("enc")
    x, y = dp // SIDE, dp % SIDE
    z, c = e // 2, e % 2

    def device(dx=0, dy=0, dz=0, dc=0):
        return (
            ((x + dx + SIDE) % SIDE) * SIDE + (y + dy + SIDE) % SIDE,
            ((z + dz + DEPTH) % DEPTH) * 2 + (c + dc) % 2,
        )

    def remote(src, dst, sems, index, to):
        return pltpu.make_async_remote_copy(
            src_ref=src,
            dst_ref=dst,
            send_sem=sems.at[(0,) + index],
            recv_sem=sems.at[(1,) + index],
            device_id=to,
            device_id_type=pl.DeviceIdType.MESH,
        )

    right_x, left_x = (x + 1) % SIDE, (x + 3) % SIDE
    far_x = (x + 2) % SIDE
    dp_steps = [(i, j) for i in (2, 1, 3, 0) for j in (2, 1, 3, 0) if (i, j) != (0, 0)]
    enc_steps = [(i, j) for i in (0, 1, 7, 2, 6, 3, 5, 4) for j in (0, 1)][1:]

    load_targets = pltpu.make_async_copy(targets, own_targets, local_sem.at[0])
    load_encoded = pltpu.make_async_copy(encoded, enc_all.at[x, y], local_sem.at[1])
    load_k = pltpu.make_async_copy(key_weight, weight_k, local_sem.at[2])
    load_v = pltpu.make_async_copy(value_weight, weight_v, local_sem.at[3])
    load_q = pltpu.make_async_copy(query_weight.at[:, y], weight_q.at[y], local_sem.at[4])
    load_o = pltpu.make_async_copy(
        output_weight.at[:, pl.ds(pl.multiple_of(x * 1024, 1024), 1024)],
        weight_o.at[x],
        local_sem.at[5],
    )
    load_targets.start()
    load_encoded.start()

    barrier = pltpu.get_barrier_semaphore()
    for i, j in dp_steps:
        pl.semaphore_signal(
            barrier, inc=1, device_id=device(dx=i, dy=j), device_id_type=pl.DeviceIdType.MESH
        )
    for i, j in enc_steps:
        pl.semaphore_signal(
            barrier, inc=1, device_id=device(dz=i, dc=j), device_id_type=pl.DeviceIdType.MESH
        )
    load_targets.wait()
    owners = [slot[e * TILES + i] // TILES for i in range(TILES)]

    def tile_copy(rank):
        i, j = enc_steps[rank - 1]
        return remote(
            sent_tiles.at[rank], came_tiles.at[rank], tile_sem, (rank,), device(dz=i, dc=j)
        )

    def tile_for(peer):
        found = jnp.int32(0)
        for i in range(1, TILES):
            found = jnp.where(owners[i] == peer, i, found)
        return own_targets[found]

    for rank in range(1, ENC_PEERS):
        i, j = enc_steps[rank - 1]
        sent_tiles[rank] = tile_for(device(dz=i, dc=j)[1])
    came_tiles[0] = tile_for(e)

    pl.semaphore_wait(barrier, len(dp_steps) + len(enc_steps))
    for rank in range(1, NEAR):
        tile_copy(rank).start()

    upper, lower = pl.ds(0, SPLIT), pl.ds(SPLIT, TILE - SPLIT)

    def enc_first(i):
        return (
            remote(
                encoded.at[upper], enc_all.at[x, y, upper], enc_sem, (0, i), device(dx=i)
            ),
            remote(
                encoded.at[lower], enc_all.at[x, y, lower], enc_sem, (1, i), device(dy=i)
            ),
        )

    def enc_second(i):
        column, line = enc_all.at[:, y, upper], enc_all.at[x, :, lower]
        return (
            remote(column, column, enc_sem, (2, i), device(dy=i)),
            remote(line, line, enc_sem, (3, i), device(dx=i)),
        )

    for i in (2, 1, 3):
        for copy in enc_first(i):
            copy.start()

    def wq_copy(j):
        part = pl.ds(2 * c, 2)
        return remote(
            query_weight.at[part, (y + j) % SIDE],
            weight_q.at[y, part],
            wq_sem,
            (j,),
            device(dy=j),
        )

    def wo_copy(i):
        part = pl.ds(pl.multiple_of(c * TILE, TILE), TILE)
        return remote(
            output_weight.at[part, pl.ds(pl.multiple_of(((x + i) % SIDE) * 1024, 1024), 1024)],
            weight_o.at[x, part],
            wo_sem,
            (i,),
            device(dx=i),
        )

    load_k.start()
    load_v.start()
    load_q.start()
    load_o.start()
    load_encoded.wait()
    for i in (1, 3, 2):
        for copy in enc_first(i):
            copy.wait_recv()
    for i in (2, 1, 3):
        for copy in enc_second(i):
            copy.start()
    for i in (2, 1, 3):
        wq_copy(i).start()
        wo_copy(i).start()
    for rank in range(NEAR, ENC_PEERS):
        tile_copy(rank).start()

    load_k.wait()
    load_v.wait()
    for i in (1, 3, 2):
        for copy in enc_second(i):
            copy.wait_recv()

    def project(weight):
        total = jnp.zeros((TILE, HD), F32)
        for i in range(SIDE):
            part = jnp.zeros((TILE, HD), F32)
            for j in range(SIDE):
                part = part + jnp.dot(
                    enc_all[i, j], weight[i * SIDE + j], preferred_element_type=F32
                )
            total = total + part
        return total.astype(BF)

    def kv_block(step):
        return ((z + step + DEPTH) % DEPTH) * 2 + c

    def kv_copy(step, way, part):
        block = kv_block(-step * way)
        ref = kv.at[block, part]
        return remote(ref, ref, kv_sem, (step, 0 if way > 0 else 1, part), device(dz=way))

    def kv_pair(step):
        block = kv_block(step)
        return remote(kv.at[block], kv.at[block], kvp_sem, ((step + DEPTH) % DEPTH,), device(dc=1))

    for part, weight in ((0, weight_k), (1, weight_v)):
        kv[e, part] = project(weight)
        kv_copy(0, 1, part).start()
        kv_copy(0, -1, part).start()
    kv_pair(0).start()

    def wq_pair(j):
        block = (y + SIDE - j) % SIDE
        part = pl.ds(2 * c, 2)
        ref = weight_q.at[block, part]
        return remote(ref, ref, pair_sem, (j,), device(dc=1))

    def wo_pair(i):
        block = (x + SIDE - i) % SIDE
        part = pl.ds(pl.multiple_of(c * TILE, TILE), TILE)
        ref = weight_o.at[block, part]
        return remote(ref, ref, pair_sem, (SIDE + i,), device(dc=1))

    lanes = lax.broadcasted_iota(jnp.int32, (TILE, TILE), 1)
    eye = lax.broadcasted_iota(jnp.int32, (TILE, TILE), 0) == lanes

    def to_row(column):
        return jnp.sum(jnp.where(eye, column, 0.0), axis=0, keepdims=True)

    def to_column(row):
        return jnp.sum(jnp.where(eye, row, 0.0), axis=1, keepdims=True)

    slots = slot_row[...]
    first_lane = lax.broadcasted_iota(jnp.int32, (1, TILE), 1)
    slot_sources = [
        jnp.max(jnp.where(slots == e * TILES + s, first_lane, 0)) for s in range(TILES)
    ]

    def rank_of(source):
        home = source // TILES
        gap = (z - home // 2 + DEPTH) % DEPTH
        place = jnp.where(gap <= DEPTH // 2, jnp.maximum(2 * gap - 1, 0), 2 * (DEPTH - gap))
        return 2 * place + jnp.where(home % 2 == c, 0, 1)

    ranks = [rank_of(source) for source in slot_sources]
    places = []
    for s in range(TILES):
        place = jnp.int32(0)
        for other in range(TILES):
            if other != s:
                place = place + jnp.where(ranks[other] < ranks[s], 1, 0)
        places.append(place)

    def of_tile(values, t):
        value = jnp.int32(0)
        for s in range(TILES):
            value = jnp.where(places[s] == t, values[s], value)
        return value

    gain_two = gain[pl.ds(2 * dp, 2)]
    gain_row = jnp.concatenate([gain_two[0:1], gain_two[1:2]], axis=1)

    def gather_copy(buf, sems, t, way):
        ref = buf.at[t, x]
        return remote(ref, ref, sems, (t, 0 if way > 0 else 1), device(dx=way))

    def pick(t):
        rank = of_tile(ranks, t)
        picked = came_tiles[t]
        for more in range(1, TILES + 1):
            picked = jnp.where(rank == t + more, came_tiles[t + more], picked)
        picked = picked.astype(F32)
        rows_q[t, x] = (picked * gain_row).astype(BF)
        gather_copy(rows_q, gather_q_sem, t, 1).start()
        gather_copy(rows_q, gather_q_sem, t, -1).start()
        squares[t // BATCH, dp, pl.ds(t % BATCH, 1)] = to_row(
            jnp.sum(picked * picked, axis=1, keepdims=True)
        )

    def sq_copy(batch, i, j):
        ref = squares.at[batch, dp]
        return remote(ref, ref, sq_sem, (batch, i * SIDE + j), device(dx=i, dy=j))

    def pass_copy(buf, sems, t, way):
        block = left_x if way > 0 else right_x
        part = pl.ds(0 if way > 0 else HALF, HALF)
        ref = buf.at[t, block, part]
        return remote(ref, ref, sems, (t, 0 if way > 0 else 1), device(dx=way))

    def pass_on(buf, first_sems, sems, t):
        gather_copy(buf, first_sems, t, 1).wait_recv()
        pass_copy(buf, sems, t, 1).start()
        gather_copy(buf, first_sems, t, -1).wait_recv()
        pass_copy(buf, sems, t, -1).start()

    def far_copy(far, half, sems, t, way):
        part = 0 if way > 0 else 1
        return remote(
            far.at[t, pl.ds(part * HALF, HALF)], half.at[t, part], sems, (t, part), device(dy=way)
        )

    def multiply(buf, sems, weight_block, kept, far, half, far_sems, t):
        pass_copy(buf, sems, t, 1).wait_recv()
        pass_copy(buf, sems, t, -1).wait_recv()
        rows = [buf[t, i] for i in range(SIDE)]

        def block(step):
            n = (y + step) % SIDE
            total = jnp.dot(rows[0], weight_block(0, n), preferred_element_type=F32)
            for i in range(1, SIDE):
                total = total + jnp.dot(rows[i], weight_block(i, n), preferred_element_type=F32)
            return total

        far[t] = block(2).astype(BF)
        far_copy(far, half, far_sems, t, 1).start()
        far_copy(far, half, far_sems, t, -1).start()
        kept[t, 0] = block(1)
        kept[t, 1] = block(3)
        kept[t, 2] = block(0)

    def near_copy(near, total, sems, t, way):
        part = 0 if way > 0 else 1
        return remote(near.at[t, part], total.at[t, part], sems, (t, part), device(dy=way))

    def add_far(kept, far, half, far_sems, near, total, near_sems, t):
        far_copy(far, half, far_sems, t, 1).wait_recv()
        near[t, 0, :HALF] = (kept[t, 0, :HALF] + half[t, 0].astype(F32)).astype(BF)
        near[t, 0, HALF:] = kept[t, 0, HALF:].astype(BF)
        near_copy(near, total, near_sems, t, 1).start()
        far_copy(far, half, far_sems, t, -1).wait_recv()
        near[t, 1, :HALF] = kept[t, 1, :HALF].astype(BF)
        near[t, 1, HALF:] = (kept[t, 1, HALF:] + half[t, 1].astype(F32)).astype(BF)
        near_copy(near, total, near_sems, t, -1).start()

    def finish(kept, near, total, near_sems, t):
        near_copy(near, total, near_sems, t, 1).wait_recv()
        near_copy(near, total, near_sems, t, -1).wait_recv()
        return kept[t, 2] + total[t, 0].astype(F32) + total[t, 1].astype(F32)

    def wq_block(i, n):
        return weight_q[n, i]

    def wo_block(i, n):
        return weight_o[i, :, pl.ds(pl.multiple_of(n * HD, HD), HD)]

    enc_row = jnp.concatenate([encoder_segment[i : i + 1] for i in range(ENC_PEERS)], axis=1)

    def attend(t):
        batch, row = t // BATCH, pl.ds(t % BATCH, 1)
        total = squares[batch, 0, row]
        for i in range(1, SIDE * SIDE):
            total = total + squares[batch, i, row]
        scale = to_column(lax.rsqrt(total * (1.0 / FEATURES) + 1e-6))
        queries = (finish(kept_q, near_q, sum_q, near_q_sem, t) * scale).astype(BF)
        segment = to_column(target_segment[pl.ds(of_tile(slot_sources, t), 1)].astype(F32)).astype(jnp.int32)
        keys = kv[:, 0].reshape(ENC_PEERS * TILE, HD)
        values = kv[:, 1].reshape(ENC_PEERS * TILE, HD)
        scores = lax.dot_general(
            queries, keys, (((1,), (1,)), ((), ())), preferred_element_type=F32
        )
        allowed = segment == enc_row
        scores = jnp.where(allowed, scores, -1e30)
        top = jnp.max(scores, axis=-1, keepdims=True)
        weights = jnp.exp(scores - top)
        denominator = jnp.sum(weights, axis=-1, keepdims=True)
        summed = jnp.dot(weights.astype(BF), values, preferred_element_type=F32)
        rows_o[t, x] = (summed / denominator).astype(BF)
        gather_copy(rows_o, gather_o_sem, t, 1).start()
        gather_copy(rows_o, gather_o_sem, t, -1).start()

    def out_copy(t):
        return pltpu.make_async_copy(
            out_tiles.at[t], out.at[pl.ds(pl.multiple_of(t * TILE, TILE), TILE)], out_sem.at[t]
        )

    def kv_step(h):
        for part in (0, 1):
            for way in (1, -1):
                kv_copy(h - 1, way, part).wait_recv()
                if h < 3 or part == (0 if way > 0 else 1):
                    kv_copy(h, way, part).start()
        kv_pair(-h).start()
        kv_pair(h).start()

    def turn(t, carry):
        def stage(late, body):
            tile = t - late

            @pl.when((tile >= 0) & (tile < TILES))
            def _():
                body(tile)

        def once(at, body):
            pl.when(t == at)(body)

        def pass_wq():
            for i in (1, 3, 2):
                wq_copy(i).wait()
                wq_pair(i).start()

        def pass_wo():
            for i in (1, 3, 2):
                wo_copy(i).wait()
                wo_pair(i).start()

        def wait_wq():
            load_q.wait()
            for i in (1, 3, 2):
                wq_pair(i).wait()

        def wait_wo():
            load_o.wait()
            for i in (1, 3, 2):
                wo_pair(i).wait()

        def last_kv():
            kv_copy(3, 1, 0).wait_recv()
            kv_copy(3, -1, 1).wait_recv()
            kv_pair(4).start()

        def wait_kv():
            for h in range(DEPTH):
                kv_pair(h).wait_recv()

        def send_squares(batch):
            for i, j in dp_steps:
                sq_copy(batch, i, j).start()

        def wait_squares(batch):
            for i, j in dp_steps:
                sq_copy(batch, i, j).wait()

        def write(tile):
            out_rows[tile] = finish(kept_o, near_o, sum_o, near_o_sem, tile).astype(BF)

        for tile in range(1, TILES):
            once(tile, tile_copy(TILES + tile).wait_recv)
        stage(0, pick)
        for batch in range(TILES // BATCH):
            once((batch + 1) * BATCH - 1, lambda batch=batch: send_squares(batch))
        once(2, pass_wq)
        stage(2, lambda i: pass_on(rows_q, gather_q_sem, pass_q_sem, i))
        once(4, wait_wq)
        stage(4, lambda i: multiply(rows_q, pass_q_sem, wq_block, kept_q, far_q, half_q, far_q_sem, i))
        stage(6, lambda i: add_far(kept_q, far_q, half_q, far_q_sem, near_q, sum_q, near_q_sem, i))
        once(2, lambda: kv_step(1))
        once(4, lambda: kv_step(2))
        once(6, lambda: kv_step(3))
        once(7, last_kv)
        once(ATTEND, wait_kv)
        for batch in range(TILES // BATCH):
            once(ATTEND + batch * BATCH, lambda batch=batch: wait_squares(batch))
        stage(ATTEND, attend)
        once(7, pass_wo)
        stage(ATTEND + 2, lambda i: pass_on(rows_o, gather_o_sem, pass_o_sem, i))
        once(ATTEND + 4, wait_wo)
        stage(ATTEND + 4, lambda i: multiply(rows_o, pass_o_sem, wo_block, kept_o, far_o, half_o, far_o_sem, i))
        stage(ATTEND + 6, lambda i: add_far(kept_o, far_o, half_o, far_o_sem, near_o, sum_o, near_o_sem, i))
        stage(ATTEND + 8, write)
        return carry

    for rank in range(1, TILES + 1):
        tile_copy(rank).wait_recv()
    lax.fori_loop(0, TILES + ATTEND + 8, turn, 0)

    for s in range(TILES):
        out_tiles[s] = out_rows[places[s]]
        out_copy(s).start()

    for rank in range(1, ENC_PEERS):
        tile_copy(rank).wait_send()
    for i in (1, 2, 3):
        for copy in enc_first(i) + enc_second(i):
            copy.wait_send()
    for h in range(3):
        for part in (0, 1):
            kv_copy(h, 1, part).wait_send()
            kv_copy(h, -1, part).wait_send()
    kv_copy(3, 1, 0).wait_send()
    kv_copy(3, -1, 1).wait_send()
    for h in range(DEPTH):
        kv_pair(h).wait_send()

    def drain(t, carry):
        for way in (1, -1):
            gather_copy(rows_q, gather_q_sem, t, way).wait_send()
            gather_copy(rows_o, gather_o_sem, t, way).wait_send()
            pass_copy(rows_q, pass_q_sem, t, way).wait_send()
            pass_copy(rows_o, pass_o_sem, t, way).wait_send()
            far_copy(far_q, half_q, far_q_sem, t, way).wait_send()
            far_copy(far_o, half_o, far_o_sem, t, way).wait_send()
            near_copy(near_q, sum_q, near_q_sem, t, way).wait_send()
            near_copy(near_o, sum_o, near_o_sem, t, way).wait_send()
        out_copy(t).wait()
        return carry

    lax.fori_loop(0, TILES, drain, 0)


def local(
    targets,
    encoded,
    norm_gain,
    query_weight,
    key_weight,
    value_weight,
    output_weight,
    target_segment,
    encoder_segment,
    tile_slot,
):
    any_space = pl.BlockSpec(memory_space=pl.ANY)
    vmem = pl.BlockSpec(memory_space=pltpu.VMEM)
    smem = pl.BlockSpec(memory_space=pltpu.SMEM)
    sem = pltpu.SemaphoreType.DMA
    tile = (TILE, HD)
    scratch = [
        pltpu.VMEM((TILES,) + tile, BF),
        pltpu.VMEM((ENC_PEERS,) + tile, BF),
        pltpu.VMEM((ENC_PEERS,) + tile, BF),
        pltpu.VMEM((SIDE, SIDE) + tile, BF),
        pltpu.VMEM((ENC_PEERS, HD, HD), BF),
        pltpu.VMEM((ENC_PEERS, HD, HD), BF),
        pltpu.VMEM((SIDE, SIDE, HD, HD), BF),
        pltpu.VMEM((SIDE, HD, SIDE * HD), BF),
        pltpu.VMEM((ENC_PEERS, 2) + tile, BF),
        pltpu.VMEM((TILES // BATCH, SIDE * SIDE, TILES, TILE), F32),
        pltpu.VMEM((TILES, SIDE) + tile, BF),
        pltpu.VMEM((TILES, SIDE) + tile, BF),
        pltpu.VMEM((TILES, 3) + tile, F32),
        pltpu.VMEM((TILES, 3) + tile, F32),
        pltpu.VMEM((TILES,) + tile, BF),
        pltpu.VMEM((TILES,) + tile, BF),
        pltpu.VMEM((TILES, 2, HALF, HD), BF),
        pltpu.VMEM((TILES, 2, HALF, HD), BF),
        pltpu.VMEM((TILES, 2) + tile, BF),
        pltpu.VMEM((TILES, 2) + tile, BF),
        pltpu.VMEM((TILES, 2) + tile, BF),
        pltpu.VMEM((TILES, 2) + tile, BF),
        pltpu.VMEM((TILES,) + tile, BF),
        pltpu.VMEM((TILES,) + tile, BF),
        sem((6,)),
        sem((2, 4, SIDE)),
        sem((2, ENC_PEERS)),
        sem((2, SIDE)),
        sem((2, SIDE)),
        sem((2, 2 * SIDE)),
        sem((2, 4, 2, 2)),
        sem((2, DEPTH)),
        sem((2, TILES // BATCH, SIDE * SIDE)),
        sem((2, TILES, 2)),
        sem((2, TILES, 2)),
        sem((2, TILES, 2)),
        sem((2, TILES, 2)),
        sem((2, TILES, 2)),
        sem((2, TILES, 2)),
        sem((2, TILES, 2)),
        sem((2, TILES, 2)),
        sem((TILES,)),
    ]
    return pl.pallas_call(
        kernel,
        out_shape=jax.ShapeDtypeStruct((TILES * TILE, HD), BF),
        in_specs=[any_space] * 2 + [vmem] + [any_space] * 4 + [vmem] * 3 + [smem],
        out_specs=any_space,
        scratch_shapes=scratch,
        compiler_params=pltpu.CompilerParams(
            collective_id=0, has_side_effects=True, vmem_limit_bytes=56 << 20
        ),
        cost_estimate=pl.CostEstimate(
            flops=7_000_000_000, bytes_accessed=10_000_000, transcendentals=2_000_000
        ),
        name="cross_attention",
    )(
        targets.reshape((TILES,) + tile),
        encoded,
        norm_gain.reshape(2 * SIDE * SIDE, TILE),
        query_weight.reshape(SIDE, SIDE, HD, HD),
        key_weight.reshape(ENC_PEERS, HD, HD),
        value_weight.reshape(ENC_PEERS, HD, HD),
        output_weight,
        target_segment.reshape(-1, TILE),
        encoder_segment.reshape(-1, TILE),
        tile_slot.reshape(1, -1),
        tile_slot,
    )


def solution(mesh):
    return jax.shard_map(
        local,
        mesh=mesh,
        in_specs=(
            P("enc", "dp"),
            P("enc", "dp"),
            P(),
            P(None, "dp"),
            P(None, "dp"),
            P(None, "dp"),
            P("dp", None),
            P(),
            P(),
            P(),
        ),
        out_specs=P("enc", "dp"),
        check_vma=False,
    )
```

```python
import jax
import jax.numpy as jnp
from jax import lax
from jax.experimental import pallas as pl
from jax.experimental.pallas import tpu as pltpu
from jax.sharding import PartitionSpec as P

HD = 256
TILE = 128
TILES = 8
HALF = TILE // 2
SIDE = 4
DEPTH = 8
ENC_PEERS = 16
BATCH = 8
NEAR = 10
SPLIT = 32
ATTEND = 8
FEATURES = 4096
BF = jnp.bfloat16
F32 = jnp.float32


def kernel(
    targets,
    encoded,
    gain,
    query_weight,
    key_weight,
    value_weight,
    output_weight,
    target_segment,
    encoder_segment,
    slot_row,
    slot,
    out,
    own_targets,
    sent_tiles,
    came_tiles,
    enc_all,
    weight_k,
    weight_v,
    weight_q,
    weight_o,
    kv,
    squares,
    rows_q,
    rows_o,
    kept_q,
    kept_o,
    far_q,
    far_o,
    half_q,
    half_o,
    near_q,
    near_o,
    sum_q,
    sum_o,
    out_rows,
    out_tiles,
    local_sem,
    enc_sem,
    tile_sem,
    wq_sem,
    wo_sem,
    pair_sem,
    kv_sem,
    kvp_sem,
    sq_sem,
    gather_q_sem,
    gather_o_sem,
    pass_q_sem,
    pass_o_sem,
    far_q_sem,
    far_o_sem,
    near_q_sem,
    near_o_sem,
    out_sem,
):
    dp = lax.axis_index("dp")
    e = lax.axis_index("enc")
    x, y = dp // SIDE, dp % SIDE
    z, c = e // 2, e % 2

    def device(dx=0, dy=0, dz=0, dc=0):
        return (
            ((x + dx + SIDE) % SIDE) * SIDE + (y + dy + SIDE) % SIDE,
            ((z + dz + DEPTH) % DEPTH) * 2 + (c + dc) % 2,
        )

    def remote(src, dst, sems, index, to):
        return pltpu.make_async_remote_copy(
            src_ref=src,
            dst_ref=dst,
            send_sem=sems.at[(0,) + index],
            recv_sem=sems.at[(1,) + index],
            device_id=to,
            device_id_type=pl.DeviceIdType.MESH,
        )

    right_x, left_x = (x + 1) % SIDE, (x + 3) % SIDE
    far_x = (x + 2) % SIDE
    dp_steps = [(i, j) for i in (2, 1, 3, 0) for j in (2, 1, 3, 0) if (i, j) != (0, 0)]
    enc_steps = [(i, j) for i in (0, 1, 7, 2, 6, 3, 5, 4) for j in (0, 1)][1:]

    load_targets = pltpu.make_async_copy(targets, own_targets, local_sem.at[0])
    load_encoded = pltpu.make_async_copy(encoded, enc_all.at[x, y], local_sem.at[1])
    load_k = pltpu.make_async_copy(key_weight, weight_k, local_sem.at[2])
    load_v = pltpu.make_async_copy(value_weight, weight_v, local_sem.at[3])
    load_q = pltpu.make_async_copy(query_weight.at[:, y], weight_q.at[y], local_sem.at[4])
    load_o = pltpu.make_async_copy(
        output_weight.at[:, pl.ds(pl.multiple_of(x * 1024, 1024), 1024)],
        weight_o.at[x],
        local_sem.at[5],
    )
    load_targets.start()
    load_encoded.start()

    barrier = pltpu.get_barrier_semaphore()
    for i, j in dp_steps:
        pl.semaphore_signal(
            barrier, inc=1, device_id=device(dx=i, dy=j), device_id_type=pl.DeviceIdType.MESH
        )
    for i, j in enc_steps:
        pl.semaphore_signal(
            barrier, inc=1, device_id=device(dz=i, dc=j), device_id_type=pl.DeviceIdType.MESH
        )
    pl.semaphore_wait(barrier, len(dp_steps) + len(enc_steps))

    upper, lower = pl.ds(0, SPLIT), pl.ds(SPLIT, TILE - SPLIT)

    def enc_first(i):
        return (
            remote(
                encoded.at[upper], enc_all.at[x, y, upper], enc_sem, (0, i), device(dx=i)
            ),
            remote(
                encoded.at[lower], enc_all.at[x, y, lower], enc_sem, (1, i), device(dy=i)
            ),
        )

    def enc_second(i):
        column, line = enc_all.at[:, y, upper], enc_all.at[x, :, lower]
        return (
            remote(column, column, enc_sem, (2, i), device(dy=i)),
            remote(line, line, enc_sem, (3, i), device(dx=i)),
        )

    for i in (2, 1, 3):
        for copy in enc_first(i):
            copy.start()

    load_targets.wait()
    owners = [slot[e * TILES + i] // TILES for i in range(TILES)]

    def tile_copy(rank):
        i, j = enc_steps[rank - 1]
        return remote(
            sent_tiles.at[rank], came_tiles.at[rank], tile_sem, (rank,), device(dz=i, dc=j)
        )

    def tile_for(peer):
        found = jnp.int32(0)
        for i in range(1, TILES):
            found = jnp.where(owners[i] == peer, i, found)
        return own_targets[found]

    for rank in range(1, ENC_PEERS):
        i, j = enc_steps[rank - 1]
        sent_tiles[rank] = tile_for(device(dz=i, dc=j)[1])
        if rank < NEAR:
            tile_copy(rank).start()
    came_tiles[0] = tile_for(e)

    def wq_copy(j):
        part = pl.ds(2 * c, 2)
        return remote(
            query_weight.at[part, (y + j) % SIDE],
            weight_q.at[y, part],
            wq_sem,
            (j,),
            device(dy=j),
        )

    def wo_copy(i):
        part = pl.ds(pl.multiple_of(c * TILE, TILE), TILE)
        return remote(
            output_weight.at[part, pl.ds(pl.multiple_of(((x + i) % SIDE) * 1024, 1024), 1024)],
            weight_o.at[x, part],
            wo_sem,
            (i,),
            device(dx=i),
        )

    load_k.start()
    load_v.start()
    load_q.start()
    load_o.start()
    load_encoded.wait()
    for i in (1, 3, 2):
        for copy in enc_first(i):
            copy.wait_recv()
    for i in (2, 1, 3):
        for copy in enc_second(i):
            copy.start()
    for i in (2, 1, 3):
        wq_copy(i).start()
        wo_copy(i).start()
    for rank in range(NEAR, ENC_PEERS):
        tile_copy(rank).start()

    load_k.wait()
    load_v.wait()
    for i in (1, 3, 2):
        for copy in enc_second(i):
            copy.wait_recv()

    def project(weight):
        total = jnp.zeros((TILE, HD), F32)
        for i in range(SIDE):
            part = jnp.zeros((TILE, HD), F32)
            for j in range(SIDE):
                part = part + jnp.dot(
                    enc_all[i, j], weight[i * SIDE + j], preferred_element_type=F32
                )
            total = total + part
        return total.astype(BF)

    def kv_block(step):
        return ((z + step + DEPTH) % DEPTH) * 2 + c

    def kv_copy(step, way, part):
        block = kv_block(-step * way)
        ref = kv.at[block, part]
        return remote(ref, ref, kv_sem, (step, 0 if way > 0 else 1, part), device(dz=way))

    def kv_pair(step):
        block = kv_block(step)
        return remote(kv.at[block], kv.at[block], kvp_sem, ((step + DEPTH) % DEPTH,), device(dc=1))

    for part, weight in ((0, weight_k), (1, weight_v)):
        kv[e, part] = project(weight)
        kv_copy(0, 1, part).start()
        kv_copy(0, -1, part).start()
    kv_pair(0).start()

    def wq_pair(j):
        block = (y + SIDE - j) % SIDE
        part = pl.ds(2 * c, 2)
        ref = weight_q.at[block, part]
        return remote(ref, ref, pair_sem, (j,), device(dc=1))

    def wo_pair(i):
        block = (x + SIDE - i) % SIDE
        part = pl.ds(pl.multiple_of(c * TILE, TILE), TILE)
        ref = weight_o.at[block, part]
        return remote(ref, ref, pair_sem, (SIDE + i,), device(dc=1))

    lanes = lax.broadcasted_iota(jnp.int32, (TILE, TILE), 1)
    eye = lax.broadcasted_iota(jnp.int32, (TILE, TILE), 0) == lanes

    def to_row(column):
        return jnp.sum(jnp.where(eye, column, 0.0), axis=0, keepdims=True)

    def to_column(row):
        return jnp.sum(jnp.where(eye, row, 0.0), axis=1, keepdims=True)

    slots = slot_row[...]
    first_lane = lax.broadcasted_iota(jnp.int32, (1, TILE), 1)
    slot_sources = [
        jnp.max(jnp.where(slots == e * TILES + s, first_lane, 0)) for s in range(TILES)
    ]

    def rank_of(source):
        home = source // TILES
        gap = (z - home // 2 + DEPTH) % DEPTH
        place = jnp.where(gap <= DEPTH // 2, jnp.maximum(2 * gap - 1, 0), 2 * (DEPTH - gap))
        return 2 * place + jnp.where(home % 2 == c, 0, 1)

    ranks = [rank_of(source) for source in slot_sources]
    places = []
    for s in range(TILES):
        place = jnp.int32(0)
        for other in range(TILES):
            if other != s:
                place = place + jnp.where(ranks[other] < ranks[s], 1, 0)
        places.append(place)

    def of_tile(values, t):
        value = jnp.int32(0)
        for s in range(TILES):
            value = jnp.where(places[s] == t, values[s], value)
        return value

    gain_two = gain[pl.ds(2 * dp, 2)]
    gain_row = jnp.concatenate([gain_two[0:1], gain_two[1:2]], axis=1)

    def gather_copy(buf, sems, t, way):
        ref = buf.at[t, x]
        return remote(ref, ref, sems, (t, 0 if way > 0 else 1), device(dx=way))

    def pick(t):
        rank = of_tile(ranks, t)
        picked = came_tiles[t]
        for more in range(1, TILES + 1):
            picked = jnp.where(rank == t + more, came_tiles[t + more], picked)
        picked = picked.astype(F32)
        rows_q[t, x] = (picked * gain_row).astype(BF)
        gather_copy(rows_q, gather_q_sem, t, 1).start()
        gather_copy(rows_q, gather_q_sem, t, -1).start()
        squares[t // BATCH, dp, pl.ds(t % BATCH, 1)] = to_row(
            jnp.sum(picked * picked, axis=1, keepdims=True)
        )

    def sq_copy(batch, i, j):
        ref = squares.at[batch, dp]
        return remote(ref, ref, sq_sem, (batch, i * SIDE + j), device(dx=i, dy=j))

    def pass_copy(buf, sems, t, way):
        block = left_x if way > 0 else right_x
        part = pl.ds(0 if way > 0 else HALF, HALF)
        ref = buf.at[t, block, part]
        return remote(ref, ref, sems, (t, 0 if way > 0 else 1), device(dx=way))

    def pass_on(buf, first_sems, sems, t):
        gather_copy(buf, first_sems, t, 1).wait_recv()
        pass_copy(buf, sems, t, 1).start()
        gather_copy(buf, first_sems, t, -1).wait_recv()
        pass_copy(buf, sems, t, -1).start()

    def far_copy(far, half, sems, t, way):
        part = 0 if way > 0 else 1
        return remote(
            far.at[t, pl.ds(part * HALF, HALF)], half.at[t, part], sems, (t, part), device(dy=way)
        )

    def multiply(buf, sems, weight_block, kept, far, half, far_sems, t):
        pass_copy(buf, sems, t, 1).wait_recv()
        pass_copy(buf, sems, t, -1).wait_recv()
        rows = [buf[t, i] for i in range(SIDE)]

        def block(step):
            n = (y + step) % SIDE
            total = jnp.dot(rows[0], weight_block(0, n), preferred_element_type=F32)
            for i in range(1, SIDE):
                total = total + jnp.dot(rows[i], weight_block(i, n), preferred_element_type=F32)
            return total

        far[t] = block(2).astype(BF)
        far_copy(far, half, far_sems, t, 1).start()
        far_copy(far, half, far_sems, t, -1).start()
        kept[t, 0] = block(1)
        kept[t, 1] = block(3)
        kept[t, 2] = block(0)

    def near_copy(near, total, sems, t, way):
        part = 0 if way > 0 else 1
        return remote(near.at[t, part], total.at[t, part], sems, (t, part), device(dy=way))

    def add_far(kept, far, half, far_sems, near, total, near_sems, t):
        far_copy(far, half, far_sems, t, 1).wait_recv()
        near[t, 0, :HALF] = (kept[t, 0, :HALF] + half[t, 0].astype(F32)).astype(BF)
        near[t, 0, HALF:] = kept[t, 0, HALF:].astype(BF)
        near_copy(near, total, near_sems, t, 1).start()
        far_copy(far, half, far_sems, t, -1).wait_recv()
        near[t, 1, :HALF] = kept[t, 1, :HALF].astype(BF)
        near[t, 1, HALF:] = (kept[t, 1, HALF:] + half[t, 1].astype(F32)).astype(BF)
        near_copy(near, total, near_sems, t, -1).start()

    def finish(kept, near, total, near_sems, t):
        near_copy(near, total, near_sems, t, 1).wait_recv()
        near_copy(near, total, near_sems, t, -1).wait_recv()
        return kept[t, 2] + total[t, 0].astype(F32) + total[t, 1].astype(F32)

    def wq_block(i, n):
        return weight_q[n, i]

    def wo_block(i, n):
        return weight_o[i, :, pl.ds(pl.multiple_of(n * HD, HD), HD)]

    enc_row = jnp.concatenate([encoder_segment[i : i + 1] for i in range(ENC_PEERS)], axis=1)

    def attend(t):
        batch, row = t // BATCH, pl.ds(t % BATCH, 1)
        total = squares[batch, 0, row]
        for i in range(1, SIDE * SIDE):
            total = total + squares[batch, i, row]
        scale = to_column(lax.rsqrt(total * (1.0 / FEATURES) + 1e-6))
        queries = (finish(kept_q, near_q, sum_q, near_q_sem, t) * scale).astype(BF)
        segment = to_column(target_segment[pl.ds(of_tile(slot_sources, t), 1)].astype(F32)).astype(jnp.int32)
        keys = kv[:, 0].reshape(ENC_PEERS * TILE, HD)
        values = kv[:, 1].reshape(ENC_PEERS * TILE, HD)
        scores = lax.dot_general(
            queries, keys, (((1,), (1,)), ((), ())), preferred_element_type=F32
        )
        allowed = segment == enc_row
        scores = jnp.where(allowed, scores, -1e30)
        top = jnp.max(scores, axis=-1, keepdims=True)
        weights = jnp.exp(scores - top)
        denominator = jnp.sum(weights, axis=-1, keepdims=True)
        summed = jnp.dot(weights.astype(BF), values, preferred_element_type=F32)
        rows_o[t, x] = (summed / denominator).astype(BF)
        gather_copy(rows_o, gather_o_sem, t, 1).start()
        gather_copy(rows_o, gather_o_sem, t, -1).start()

    def out_copy(t):
        return pltpu.make_async_copy(
            out_tiles.at[t], out.at[pl.ds(pl.multiple_of(t * TILE, TILE), TILE)], out_sem.at[t]
        )

    def kv_step(h):
        for part in (0, 1):
            for way in (1, -1):
                kv_copy(h - 1, way, part).wait_recv()
                if h < 3 or part == (0 if way > 0 else 1):
                    kv_copy(h, way, part).start()
        kv_pair(-h).start()
        kv_pair(h).start()

    def turn(t, carry):
        def stage(late, body):
            tile = t - late

            @pl.when((tile >= 0) & (tile < TILES))
            def _():
                body(tile)

        def once(at, body):
            pl.when(t == at)(body)

        def pass_wq():
            for i in (1, 3, 2):
                wq_copy(i).wait()
                wq_pair(i).start()

        def pass_wo():
            for i in (1, 3, 2):
                wo_copy(i).wait()
                wo_pair(i).start()

        def wait_wq():
            load_q.wait()
            for i in (1, 3, 2):
                wq_pair(i).wait()

        def wait_wo():
            load_o.wait()
            for i in (1, 3, 2):
                wo_pair(i).wait()

        def last_kv():
            kv_copy(3, 1, 0).wait_recv()
            kv_copy(3, -1, 1).wait_recv()
            kv_pair(4).start()

        def wait_kv():
            for h in range(DEPTH):
                kv_pair(h).wait_recv()

        def send_squares(batch):
            for i, j in dp_steps:
                sq_copy(batch, i, j).start()

        def wait_squares(batch):
            for i, j in dp_steps:
                sq_copy(batch, i, j).wait()

        def write(tile):
            out_rows[tile] = finish(kept_o, near_o, sum_o, near_o_sem, tile).astype(BF)

        for tile in range(1, TILES):
            once(tile, tile_copy(TILES + tile).wait_recv)
        stage(0, pick)
        for batch in range(TILES // BATCH):
            once((batch + 1) * BATCH - 1, lambda batch=batch: send_squares(batch))
        once(2, pass_wq)
        stage(2, lambda i: pass_on(rows_q, gather_q_sem, pass_q_sem, i))
        once(4, wait_wq)
        stage(4, lambda i: multiply(rows_q, pass_q_sem, wq_block, kept_q, far_q, half_q, far_q_sem, i))
        stage(6, lambda i: add_far(kept_q, far_q, half_q, far_q_sem, near_q, sum_q, near_q_sem, i))
        once(2, lambda: kv_step(1))
        once(4, lambda: kv_step(2))
        once(6, lambda: kv_step(3))
        once(7, last_kv)
        once(ATTEND, wait_kv)
        for batch in range(TILES // BATCH):
            once(ATTEND + batch * BATCH, lambda batch=batch: wait_squares(batch))
        stage(ATTEND, attend)
        once(7, pass_wo)
        stage(ATTEND + 2, lambda i: pass_on(rows_o, gather_o_sem, pass_o_sem, i))
        once(ATTEND + 4, wait_wo)
        stage(ATTEND + 4, lambda i: multiply(rows_o, pass_o_sem, wo_block, kept_o, far_o, half_o, far_o_sem, i))
        stage(ATTEND + 6, lambda i: add_far(kept_o, far_o, half_o, far_o_sem, near_o, sum_o, near_o_sem, i))
        stage(ATTEND + 8, write)
        return carry

    for rank in range(1, TILES + 1):
        tile_copy(rank).wait_recv()
    lax.fori_loop(0, TILES + ATTEND + 8, turn, 0)

    for s in range(TILES):
        out_tiles[s] = out_rows[places[s]]
        out_copy(s).start()

    for rank in range(1, ENC_PEERS):
        tile_copy(rank).wait_send()
    for i in (1, 2, 3):
        for copy in enc_first(i) + enc_second(i):
            copy.wait_send()
    for h in range(3):
        for part in (0, 1):
            kv_copy(h, 1, part).wait_send()
            kv_copy(h, -1, part).wait_send()
    kv_copy(3, 1, 0).wait_send()
    kv_copy(3, -1, 1).wait_send()
    for h in range(DEPTH):
        kv_pair(h).wait_send()

    def drain(t, carry):
        for way in (1, -1):
            gather_copy(rows_q, gather_q_sem, t, way).wait_send()
            gather_copy(rows_o, gather_o_sem, t, way).wait_send()
            pass_copy(rows_q, pass_q_sem, t, way).wait_send()
            pass_copy(rows_o, pass_o_sem, t, way).wait_send()
            far_copy(far_q, half_q, far_q_sem, t, way).wait_send()
            far_copy(far_o, half_o, far_o_sem, t, way).wait_send()
            near_copy(near_q, sum_q, near_q_sem, t, way).wait_send()
            near_copy(near_o, sum_o, near_o_sem, t, way).wait_send()
        out_copy(t).wait()
        return carry

    lax.fori_loop(0, TILES, drain, 0)


def local(
    targets,
    encoded,
    norm_gain,
    query_weight,
    key_weight,
    value_weight,
    output_weight,
    target_segment,
    encoder_segment,
    tile_slot,
):
    any_space = pl.BlockSpec(memory_space=pl.ANY)
    vmem = pl.BlockSpec(memory_space=pltpu.VMEM)
    smem = pl.BlockSpec(memory_space=pltpu.SMEM)
    sem = pltpu.SemaphoreType.DMA
    tile = (TILE, HD)
    scratch = [
        pltpu.VMEM((TILES,) + tile, BF),
        pltpu.VMEM((ENC_PEERS,) + tile, BF),
        pltpu.VMEM((ENC_PEERS,) + tile, BF),
        pltpu.VMEM((SIDE, SIDE) + tile, BF),
        pltpu.VMEM((ENC_PEERS, HD, HD), BF),
        pltpu.VMEM((ENC_PEERS, HD, HD), BF),
        pltpu.VMEM((SIDE, SIDE, HD, HD), BF),
        pltpu.VMEM((SIDE, HD, SIDE * HD), BF),
        pltpu.VMEM((ENC_PEERS, 2) + tile, BF),
        pltpu.VMEM((TILES // BATCH, SIDE * SIDE, TILES, TILE), F32),
        pltpu.VMEM((TILES, SIDE) + tile, BF),
        pltpu.VMEM((TILES, SIDE) + tile, BF),
        pltpu.VMEM((TILES, 3) + tile, F32),
        pltpu.VMEM((TILES, 3) + tile, F32),
        pltpu.VMEM((TILES,) + tile, BF),
        pltpu.VMEM((TILES,) + tile, BF),
        pltpu.VMEM((TILES, 2, HALF, HD), BF),
        pltpu.VMEM((TILES, 2, HALF, HD), BF),
        pltpu.VMEM((TILES, 2) + tile, BF),
        pltpu.VMEM((TILES, 2) + tile, BF),
        pltpu.VMEM((TILES, 2) + tile, BF),
        pltpu.VMEM((TILES, 2) + tile, BF),
        pltpu.VMEM((TILES,) + tile, BF),
        pltpu.VMEM((TILES,) + tile, BF),
        sem((6,)),
        sem((2, 4, SIDE)),
        sem((2, ENC_PEERS)),
        sem((2, SIDE)),
        sem((2, SIDE)),
        sem((2, 2 * SIDE)),
        sem((2, 4, 2, 2)),
        sem((2, DEPTH)),
        sem((2, TILES // BATCH, SIDE * SIDE)),
        sem((2, TILES, 2)),
        sem((2, TILES, 2)),
        sem((2, TILES, 2)),
        sem((2, TILES, 2)),
        sem((2, TILES, 2)),
        sem((2, TILES, 2)),
        sem((2, TILES, 2)),
        sem((2, TILES, 2)),
        sem((TILES,)),
    ]
    return pl.pallas_call(
        kernel,
        out_shape=jax.ShapeDtypeStruct((TILES * TILE, HD), BF),
        in_specs=[any_space] * 2 + [vmem] + [any_space] * 4 + [vmem] * 3 + [smem],
        out_specs=any_space,
        scratch_shapes=scratch,
        compiler_params=pltpu.CompilerParams(
            collective_id=0, has_side_effects=True, vmem_limit_bytes=56 << 20
        ),
        cost_estimate=pl.CostEstimate(
            flops=7_000_000_000, bytes_accessed=10_000_000, transcendentals=2_000_000
        ),
        name="cross_attention",
    )(
        targets.reshape((TILES,) + tile),
        encoded,
        norm_gain.reshape(2 * SIDE * SIDE, TILE),
        query_weight.reshape(SIDE, SIDE, HD, HD),
        key_weight.reshape(ENC_PEERS, HD, HD),
        value_weight.reshape(ENC_PEERS, HD, HD),
        output_weight,
        target_segment.reshape(-1, TILE),
        encoder_segment.reshape(-1, TILE),
        tile_slot.reshape(1, -1),
        tile_slot,
    )


def solution(mesh):
    return jax.shard_map(
        local,
        mesh=mesh,
        in_specs=(
            P("enc", "dp"),
            P("enc", "dp"),
            P(),
            P(None, "dp"),
            P(None, "dp"),
            P(None, "dp"),
            P("dp", None),
            P(),
            P(),
            P(),
        ),
        out_specs=P("enc", "dp"),
        check_vma=False,
    )
```

```python
import jax
import jax.numpy as jnp
from jax import lax
from jax.experimental import pallas as pl
from jax.experimental.pallas import tpu as pltpu
from jax.sharding import PartitionSpec as P

HD = 256
TILE = 128
TILES = 8
HALF = TILE // 2
SIDE = 4
DEPTH = 8
ENC_PEERS = 16
BATCH = 8
NEAR = 10
SPLIT = 16
ATTEND = 8
FEATURES = 4096
BF = jnp.bfloat16
F32 = jnp.float32


def kernel(
    targets,
    encoded,
    gain,
    query_weight,
    key_weight,
    value_weight,
    output_weight,
    target_segment,
    encoder_segment,
    slot_row,
    slot,
    out,
    own_targets,
    sent_tiles,
    came_tiles,
    enc_all,
    weight_k,
    weight_v,
    weight_q,
    weight_o,
    kv,
    squares,
    rows_q,
    rows_o,
    kept_q,
    kept_o,
    far_q,
    far_o,
    half_q,
    half_o,
    near_q,
    near_o,
    sum_q,
    sum_o,
    out_rows,
    out_tiles,
    local_sem,
    enc_sem,
    tile_sem,
    wq_sem,
    wo_sem,
    pair_sem,
    kv_sem,
    kvp_sem,
    sq_sem,
    gather_q_sem,
    gather_o_sem,
    pass_q_sem,
    pass_o_sem,
    far_q_sem,
    far_o_sem,
    near_q_sem,
    near_o_sem,
    out_sem,
):
    dp = lax.axis_index("dp")
    e = lax.axis_index("enc")
    x, y = dp // SIDE, dp % SIDE
    z, c = e // 2, e % 2

    def device(dx=0, dy=0, dz=0, dc=0):
        return (
            ((x + dx + SIDE) % SIDE) * SIDE + (y + dy + SIDE) % SIDE,
            ((z + dz + DEPTH) % DEPTH) * 2 + (c + dc) % 2,
        )

    def remote(src, dst, sems, index, to):
        return pltpu.make_async_remote_copy(
            src_ref=src,
            dst_ref=dst,
            send_sem=sems.at[(0,) + index],
            recv_sem=sems.at[(1,) + index],
            device_id=to,
            device_id_type=pl.DeviceIdType.MESH,
        )

    right_x, left_x = (x + 1) % SIDE, (x + 3) % SIDE
    far_x = (x + 2) % SIDE
    dp_steps = [(i, j) for i in (2, 1, 3, 0) for j in (2, 1, 3, 0) if (i, j) != (0, 0)]
    enc_steps = [(i, j) for i in (0, 1, 7, 2, 6, 3, 5, 4) for j in (0, 1)][1:]

    load_targets = pltpu.make_async_copy(targets, own_targets, local_sem.at[0])
    load_encoded = pltpu.make_async_copy(encoded, enc_all.at[x, y], local_sem.at[1])
    load_k = pltpu.make_async_copy(key_weight, weight_k, local_sem.at[2])
    load_v = pltpu.make_async_copy(value_weight, weight_v, local_sem.at[3])
    load_q = pltpu.make_async_copy(query_weight.at[:, y], weight_q.at[y], local_sem.at[4])
    load_o = pltpu.make_async_copy(
        output_weight.at[:, pl.ds(pl.multiple_of(x * 1024, 1024), 1024)],
        weight_o.at[x],
        local_sem.at[5],
    )
    load_targets.start()
    load_encoded.start()

    barrier = pltpu.get_barrier_semaphore()
    for i, j in dp_steps:
        pl.semaphore_signal(
            barrier, inc=1, device_id=device(dx=i, dy=j), device_id_type=pl.DeviceIdType.MESH
        )
    for i, j in enc_steps:
        pl.semaphore_signal(
            barrier, inc=1, device_id=device(dz=i, dc=j), device_id_type=pl.DeviceIdType.MESH
        )
    pl.semaphore_wait(barrier, len(dp_steps) + len(enc_steps))

    upper, lower = pl.ds(0, SPLIT), pl.ds(SPLIT, TILE - SPLIT)

    def enc_first(i):
        return (
            remote(
                encoded.at[upper], enc_all.at[x, y, upper], enc_sem, (0, i), device(dx=i)
            ),
            remote(
                encoded.at[lower], enc_all.at[x, y, lower], enc_sem, (1, i), device(dy=i)
            ),
        )

    def enc_second(i):
        column, line = enc_all.at[:, y, upper], enc_all.at[x, :, lower]
        return (
            remote(column, column, enc_sem, (2, i), device(dy=i)),
            remote(line, line, enc_sem, (3, i), device(dx=i)),
        )

    for i in (2, 1, 3):
        for copy in enc_first(i):
            copy.start()

    load_targets.wait()
    owners = [slot[e * TILES + i] // TILES for i in range(TILES)]

    def tile_copy(rank):
        i, j = enc_steps[rank - 1]
        return remote(
            sent_tiles.at[rank], came_tiles.at[rank], tile_sem, (rank,), device(dz=i, dc=j)
        )

    def tile_for(peer):
        found = jnp.int32(0)
        for i in range(1, TILES):
            found = jnp.where(owners[i] == peer, i, found)
        return own_targets[found]

    for rank in range(1, ENC_PEERS):
        i, j = enc_steps[rank - 1]
        sent_tiles[rank] = tile_for(device(dz=i, dc=j)[1])
        if rank < NEAR:
            tile_copy(rank).start()
    came_tiles[0] = tile_for(e)

    def wq_copy(j):
        part = pl.ds(2 * c, 2)
        return remote(
            query_weight.at[part, (y + j) % SIDE],
            weight_q.at[y, part],
            wq_sem,
            (j,),
            device(dy=j),
        )

    def wo_copy(i):
        part = pl.ds(pl.multiple_of(c * TILE, TILE), TILE)
        return remote(
            output_weight.at[part, pl.ds(pl.multiple_of(((x + i) % SIDE) * 1024, 1024), 1024)],
            weight_o.at[x, part],
            wo_sem,
            (i,),
            device(dx=i),
        )

    load_k.start()
    load_v.start()
    load_q.start()
    load_o.start()
    load_encoded.wait()
    for i in (1, 3, 2):
        for copy in enc_first(i):
            copy.wait_recv()
    for i in (2, 1, 3):
        for copy in enc_second(i):
            copy.start()
    for i in (2, 1, 3):
        wq_copy(i).start()
        wo_copy(i).start()
    for rank in range(NEAR, ENC_PEERS):
        tile_copy(rank).start()

    load_k.wait()
    load_v.wait()
    for i in (1, 3, 2):
        for copy in enc_second(i):
            copy.wait_recv()

    def project(weight):
        total = jnp.zeros((TILE, HD), F32)
        for i in range(SIDE):
            part = jnp.zeros((TILE, HD), F32)
            for j in range(SIDE):
                part = part + jnp.dot(
                    enc_all[i, j], weight[i * SIDE + j], preferred_element_type=F32
                )
            total = total + part
        return total.astype(BF)

    def kv_block(step):
        return ((z + step + DEPTH) % DEPTH) * 2 + c

    def kv_copy(step, way, part):
        block = kv_block(-step * way)
        ref = kv.at[block, part]
        return remote(ref, ref, kv_sem, (step, 0 if way > 0 else 1, part), device(dz=way))

    def kv_pair(step):
        block = kv_block(step)
        return remote(kv.at[block], kv.at[block], kvp_sem, ((step + DEPTH) % DEPTH,), device(dc=1))

    for part, weight in ((0, weight_k), (1, weight_v)):
        kv[e, part] = project(weight)
        kv_copy(0, 1, part).start()
        kv_copy(0, -1, part).start()
    kv_pair(0).start()

    def wq_pair(j):
        block = (y + SIDE - j) % SIDE
        part = pl.ds(2 * c, 2)
        ref = weight_q.at[block, part]
        return remote(ref, ref, pair_sem, (j,), device(dc=1))

    def wo_pair(i):
        block = (x + SIDE - i) % SIDE
        part = pl.ds(pl.multiple_of(c * TILE, TILE), TILE)
        ref = weight_o.at[block, part]
        return remote(ref, ref, pair_sem, (SIDE + i,), device(dc=1))

    lanes = lax.broadcasted_iota(jnp.int32, (TILE, TILE), 1)
    eye = lax.broadcasted_iota(jnp.int32, (TILE, TILE), 0) == lanes

    def to_row(column):
        return jnp.sum(jnp.where(eye, column, 0.0), axis=0, keepdims=True)

    def to_column(row):
        return jnp.sum(jnp.where(eye, row, 0.0), axis=1, keepdims=True)

    slots = slot_row[...]
    first_lane = lax.broadcasted_iota(jnp.int32, (1, TILE), 1)
    slot_sources = [
        jnp.max(jnp.where(slots == e * TILES + s, first_lane, 0)) for s in range(TILES)
    ]

    def rank_of(source):
        home = source // TILES
        gap = (z - home // 2 + DEPTH) % DEPTH
        place = jnp.where(gap <= DEPTH // 2, jnp.maximum(2 * gap - 1, 0), 2 * (DEPTH - gap))
        return 2 * place + jnp.where(home % 2 == c, 0, 1)

    ranks = [rank_of(source) for source in slot_sources]
    places = []
    for s in range(TILES):
        place = jnp.int32(0)
        for other in range(TILES):
            if other != s:
                place = place + jnp.where(ranks[other] < ranks[s], 1, 0)
        places.append(place)

    def of_tile(values, t):
        value = jnp.int32(0)
        for s in range(TILES):
            value = jnp.where(places[s] == t, values[s], value)
        return value

    gain_two = gain[pl.ds(2 * dp, 2)]
    gain_row = jnp.concatenate([gain_two[0:1], gain_two[1:2]], axis=1)

    def gather_copy(buf, sems, t, way):
        ref = buf.at[t, x]
        return remote(ref, ref, sems, (t, 0 if way > 0 else 1), device(dx=way))

    def pick(t):
        rank = of_tile(ranks, t)
        picked = came_tiles[t]
        for more in range(1, TILES + 1):
            picked = jnp.where(rank == t + more, came_tiles[t + more], picked)
        picked = picked.astype(F32)
        rows_q[t, x] = (picked * gain_row).astype(BF)
        gather_copy(rows_q, gather_q_sem, t, 1).start()
        gather_copy(rows_q, gather_q_sem, t, -1).start()
        squares[t // BATCH, dp, pl.ds(t % BATCH, 1)] = to_row(
            jnp.sum(picked * picked, axis=1, keepdims=True)
        )

    def sq_copy(batch, i, j):
        ref = squares.at[batch, dp]
        return remote(ref, ref, sq_sem, (batch, i * SIDE + j), device(dx=i, dy=j))

    def pass_copy(buf, sems, t, way):
        block = left_x if way > 0 else right_x
        part = pl.ds(0 if way > 0 else HALF, HALF)
        ref = buf.at[t, block, part]
        return remote(ref, ref, sems, (t, 0 if way > 0 else 1), device(dx=way))

    def pass_on(buf, first_sems, sems, t):
        gather_copy(buf, first_sems, t, 1).wait_recv()
        pass_copy(buf, sems, t, 1).start()
        gather_copy(buf, first_sems, t, -1).wait_recv()
        pass_copy(buf, sems, t, -1).start()

    def far_copy(far, half, sems, t, way):
        part = 0 if way > 0 else 1
        return remote(
            far.at[t, pl.ds(part * HALF, HALF)], half.at[t, part], sems, (t, part), device(dy=way)
        )

    def multiply(buf, sems, weight_block, kept, far, half, far_sems, t):
        pass_copy(buf, sems, t, 1).wait_recv()
        pass_copy(buf, sems, t, -1).wait_recv()
        rows = [buf[t, i] for i in range(SIDE)]

        def block(step):
            n = (y + step) % SIDE
            total = jnp.dot(rows[0], weight_block(0, n), preferred_element_type=F32)
            for i in range(1, SIDE):
                total = total + jnp.dot(rows[i], weight_block(i, n), preferred_element_type=F32)
            return total

        far[t] = block(2).astype(BF)
        far_copy(far, half, far_sems, t, 1).start()
        far_copy(far, half, far_sems, t, -1).start()
        kept[t, 0] = block(1)
        kept[t, 1] = block(3)
        kept[t, 2] = block(0)

    def near_copy(near, total, sems, t, way):
        part = 0 if way > 0 else 1
        return remote(near.at[t, part], total.at[t, part], sems, (t, part), device(dy=way))

    def add_far(kept, far, half, far_sems, near, total, near_sems, t):
        far_copy(far, half, far_sems, t, 1).wait_recv()
        near[t, 0, :HALF] = (kept[t, 0, :HALF] + half[t, 0].astype(F32)).astype(BF)
        near[t, 0, HALF:] = kept[t, 0, HALF:].astype(BF)
        near_copy(near, total, near_sems, t, 1).start()
        far_copy(far, half, far_sems, t, -1).wait_recv()
        near[t, 1, :HALF] = kept[t, 1, :HALF].astype(BF)
        near[t, 1, HALF:] = (kept[t, 1, HALF:] + half[t, 1].astype(F32)).astype(BF)
        near_copy(near, total, near_sems, t, -1).start()

    def finish(kept, near, total, near_sems, t):
        near_copy(near, total, near_sems, t, 1).wait_recv()
        near_copy(near, total, near_sems, t, -1).wait_recv()
        return kept[t, 2] + total[t, 0].astype(F32) + total[t, 1].astype(F32)

    def wq_block(i, n):
        return weight_q[n, i]

    def wo_block(i, n):
        return weight_o[i, :, pl.ds(pl.multiple_of(n * HD, HD), HD)]

    enc_row = jnp.concatenate([encoder_segment[i : i + 1] for i in range(ENC_PEERS)], axis=1)

    def attend(t):
        batch, row = t // BATCH, pl.ds(t % BATCH, 1)
        total = squares[batch, 0, row]
        for i in range(1, SIDE * SIDE):
            total = total + squares[batch, i, row]
        scale = to_column(lax.rsqrt(total * (1.0 / FEATURES) + 1e-6))
        queries = (finish(kept_q, near_q, sum_q, near_q_sem, t) * scale).astype(BF)
        segment = to_column(target_segment[pl.ds(of_tile(slot_sources, t), 1)].astype(F32)).astype(jnp.int32)
        keys = kv[:, 0].reshape(ENC_PEERS * TILE, HD)
        values = kv[:, 1].reshape(ENC_PEERS * TILE, HD)
        scores = lax.dot_general(
            queries, keys, (((1,), (1,)), ((), ())), preferred_element_type=F32
        )
        allowed = segment == enc_row
        scores = jnp.where(allowed, scores, -1e30)
        top = jnp.max(scores, axis=-1, keepdims=True)
        weights = jnp.exp(scores - top)
        denominator = jnp.sum(weights, axis=-1, keepdims=True)
        summed = jnp.dot(weights.astype(BF), values, preferred_element_type=F32)
        rows_o[t, x] = (summed / denominator).astype(BF)
        gather_copy(rows_o, gather_o_sem, t, 1).start()
        gather_copy(rows_o, gather_o_sem, t, -1).start()

    def out_copy(t):
        return pltpu.make_async_copy(
            out_tiles.at[t], out.at[pl.ds(pl.multiple_of(t * TILE, TILE), TILE)], out_sem.at[t]
        )

    def kv_step(h):
        for part in (0, 1):
            for way in (1, -1):
                kv_copy(h - 1, way, part).wait_recv()
                if h < 3 or part == (0 if way > 0 else 1):
                    kv_copy(h, way, part).start()
        kv_pair(-h).start()
        kv_pair(h).start()

    def turn(t, carry):
        def stage(late, body):
            tile = t - late

            @pl.when((tile >= 0) & (tile < TILES))
            def _():
                body(tile)

        def once(at, body):
            pl.when(t == at)(body)

        def pass_wq():
            for i in (1, 3, 2):
                wq_copy(i).wait()
                wq_pair(i).start()

        def pass_wo():
            for i in (1, 3, 2):
                wo_copy(i).wait()
                wo_pair(i).start()

        def wait_wq():
            load_q.wait()
            for i in (1, 3, 2):
                wq_pair(i).wait()

        def wait_wo():
            load_o.wait()
            for i in (1, 3, 2):
                wo_pair(i).wait()

        def last_kv():
            kv_copy(3, 1, 0).wait_recv()
            kv_copy(3, -1, 1).wait_recv()
            kv_pair(4).start()

        def wait_kv():
            for h in range(DEPTH):
                kv_pair(h).wait_recv()

        def send_squares(batch):
            for i, j in dp_steps:
                sq_copy(batch, i, j).start()

        def wait_squares(batch):
            for i, j in dp_steps:
                sq_copy(batch, i, j).wait()

        def write(tile):
            out_rows[tile] = finish(kept_o, near_o, sum_o, near_o_sem, tile).astype(BF)

        for tile in range(1, TILES):
            once(tile, tile_copy(TILES + tile).wait_recv)
        stage(0, pick)
        for batch in range(TILES // BATCH):
            once((batch + 1) * BATCH - 1, lambda batch=batch: send_squares(batch))
        once(2, pass_wq)
        stage(2, lambda i: pass_on(rows_q, gather_q_sem, pass_q_sem, i))
        once(4, wait_wq)
        stage(4, lambda i: multiply(rows_q, pass_q_sem, wq_block, kept_q, far_q, half_q, far_q_sem, i))
        stage(6, lambda i: add_far(kept_q, far_q, half_q, far_q_sem, near_q, sum_q, near_q_sem, i))
        once(2, lambda: kv_step(1))
        once(4, lambda: kv_step(2))
        once(6, lambda: kv_step(3))
        once(7, last_kv)
        once(ATTEND, wait_kv)
        for batch in range(TILES // BATCH):
            once(ATTEND + batch * BATCH, lambda batch=batch: wait_squares(batch))
        stage(ATTEND, attend)
        once(7, pass_wo)
        stage(ATTEND + 2, lambda i: pass_on(rows_o, gather_o_sem, pass_o_sem, i))
        once(ATTEND + 4, wait_wo)
        stage(ATTEND + 4, lambda i: multiply(rows_o, pass_o_sem, wo_block, kept_o, far_o, half_o, far_o_sem, i))
        stage(ATTEND + 6, lambda i: add_far(kept_o, far_o, half_o, far_o_sem, near_o, sum_o, near_o_sem, i))
        stage(ATTEND + 8, write)
        return carry

    for rank in range(1, TILES + 1):
        tile_copy(rank).wait_recv()
    lax.fori_loop(0, TILES + ATTEND + 8, turn, 0)

    for s in range(TILES):
        out_tiles[s] = out_rows[places[s]]
        out_copy(s).start()

    for rank in range(1, ENC_PEERS):
        tile_copy(rank).wait_send()
    for i in (1, 2, 3):
        for copy in enc_first(i) + enc_second(i):
            copy.wait_send()
    for h in range(3):
        for part in (0, 1):
            kv_copy(h, 1, part).wait_send()
            kv_copy(h, -1, part).wait_send()
    kv_copy(3, 1, 0).wait_send()
    kv_copy(3, -1, 1).wait_send()
    for h in range(DEPTH):
        kv_pair(h).wait_send()

    def drain(t, carry):
        for way in (1, -1):
            gather_copy(rows_q, gather_q_sem, t, way).wait_send()
            gather_copy(rows_o, gather_o_sem, t, way).wait_send()
            pass_copy(rows_q, pass_q_sem, t, way).wait_send()
            pass_copy(rows_o, pass_o_sem, t, way).wait_send()
            far_copy(far_q, half_q, far_q_sem, t, way).wait_send()
            far_copy(far_o, half_o, far_o_sem, t, way).wait_send()
            near_copy(near_q, sum_q, near_q_sem, t, way).wait_send()
            near_copy(near_o, sum_o, near_o_sem, t, way).wait_send()
        out_copy(t).wait()
        return carry

    lax.fori_loop(0, TILES, drain, 0)


def local(
    targets,
    encoded,
    norm_gain,
    query_weight,
    key_weight,
    value_weight,
    output_weight,
    target_segment,
    encoder_segment,
    tile_slot,
):
    any_space = pl.BlockSpec(memory_space=pl.ANY)
    vmem = pl.BlockSpec(memory_space=pltpu.VMEM)
    smem = pl.BlockSpec(memory_space=pltpu.SMEM)
    sem = pltpu.SemaphoreType.DMA
    tile = (TILE, HD)
    scratch = [
        pltpu.VMEM((TILES,) + tile, BF),
        pltpu.VMEM((ENC_PEERS,) + tile, BF),
        pltpu.VMEM((ENC_PEERS,) + tile, BF),
        pltpu.VMEM((SIDE, SIDE) + tile, BF),
        pltpu.VMEM((ENC_PEERS, HD, HD), BF),
        pltpu.VMEM((ENC_PEERS, HD, HD), BF),
        pltpu.VMEM((SIDE, SIDE, HD, HD), BF),
        pltpu.VMEM((SIDE, HD, SIDE * HD), BF),
        pltpu.VMEM((ENC_PEERS, 2) + tile, BF),
        pltpu.VMEM((TILES // BATCH, SIDE * SIDE, TILES, TILE), F32),
        pltpu.VMEM((TILES, SIDE) + tile, BF),
        pltpu.VMEM((TILES, SIDE) + tile, BF),
        pltpu.VMEM((TILES, 3) + tile, F32),
        pltpu.VMEM((TILES, 3) + tile, F32),
        pltpu.VMEM((TILES,) + tile, BF),
        pltpu.VMEM((TILES,) + tile, BF),
        pltpu.VMEM((TILES, 2, HALF, HD), BF),
        pltpu.VMEM((TILES, 2, HALF, HD), BF),
        pltpu.VMEM((TILES, 2) + tile, BF),
        pltpu.VMEM((TILES, 2) + tile, BF),
        pltpu.VMEM((TILES, 2) + tile, BF),
        pltpu.VMEM((TILES, 2) + tile, BF),
        pltpu.VMEM((TILES,) + tile, BF),
        pltpu.VMEM((TILES,) + tile, BF),
        sem((6,)),
        sem((2, 4, SIDE)),
        sem((2, ENC_PEERS)),
        sem((2, SIDE)),
        sem((2, SIDE)),
        sem((2, 2 * SIDE)),
        sem((2, 4, 2, 2)),
        sem((2, DEPTH)),
        sem((2, TILES // BATCH, SIDE * SIDE)),
        sem((2, TILES, 2)),
        sem((2, TILES, 2)),
        sem((2, TILES, 2)),
        sem((2, TILES, 2)),
        sem((2, TILES, 2)),
        sem((2, TILES, 2)),
        sem((2, TILES, 2)),
        sem((2, TILES, 2)),
        sem((TILES,)),
    ]
    return pl.pallas_call(
        kernel,
        out_shape=jax.ShapeDtypeStruct((TILES * TILE, HD), BF),
        in_specs=[any_space] * 2 + [vmem] + [any_space] * 4 + [vmem] * 3 + [smem],
        out_specs=any_space,
        scratch_shapes=scratch,
        compiler_params=pltpu.CompilerParams(
            collective_id=0, has_side_effects=True, vmem_limit_bytes=56 << 20
        ),
        cost_estimate=pl.CostEstimate(
            flops=7_000_000_000, bytes_accessed=10_000_000, transcendentals=2_000_000
        ),
        name="cross_attention",
    )(
        targets.reshape((TILES,) + tile),
        encoded,
        norm_gain.reshape(2 * SIDE * SIDE, TILE),
        query_weight.reshape(SIDE, SIDE, HD, HD),
        key_weight.reshape(ENC_PEERS, HD, HD),
        value_weight.reshape(ENC_PEERS, HD, HD),
        output_weight,
        target_segment.reshape(-1, TILE),
        encoder_segment.reshape(-1, TILE),
        tile_slot.reshape(1, -1),
        tile_slot,
    )


def solution(mesh):
    return jax.shard_map(
        local,
        mesh=mesh,
        in_specs=(
            P("enc", "dp"),
            P("enc", "dp"),
            P(),
            P(None, "dp"),
            P(None, "dp"),
            P(None, "dp"),
            P("dp", None),
            P(),
            P(),
            P(),
        ),
        out_specs=P("enc", "dp"),
        check_vma=False,
    )
```
